32 devices in a mesh: sib: 4 (over z), ctx: 2 (over x), head: 4 (over y, core).
Axes of the slice: x: 2, y: 2, z: 4, core: 2. Of those that a mesh axis runs over, the one named last changes fastest.
Arguments:
- queries: bfloat16 [4, 1024, 4, 1536], P('sib', 'ctx', 'head'), may hold values from -8 to 8
- suffix_kv: bfloat16 [4, 1024, 4, 320], P('sib', 'ctx', 'head'), may hold values from -6 to 6
- prefix_kv: bfloat16 [16384, 4, 320], P(('sib', 'ctx'), 'head'), may hold values from -6 to 6
- pooling: float32 [2, 64], replicated, may hold values from 0.03 to 0.3
- gate_logits: float32 [4, 1024, 4, 24], P('sib', 'ctx', 'head'), may hold values from -6 to 6
- selected: int32 [4, 16, 4, 16], P('sib', 'ctx', 'head'), may hold values from 0 to 255, as said below
- lengths: int32 [4], P('sib'), may hold values from 128 to 1024, as said below
- w_out: bfloat16 [4096, 2560], P('head'), may hold values from -0.375 to 0.375
Outputs:
- layer_out: bfloat16 [4, 1024, 2560], P('sib', ('ctx', 'head'))
The draws below stay inside these ranges and needn't reach their ends.
Inputs may be any that keep to these rules, and one draw needn't show every extreme that they name: For each sibling and group, the 16 indices of a query block are distinct, and the query blocks of one index of ctx (8 aligned query blocks) select together at most 24 blocks, counted with repeats, among any aligned range of 32 prefix blocks; some range is selected exactly 24 times in every such run. `lengths`: some sibling has the full length 1024 and some the length 128.
All inputs are finite; a program needn't handle non-finite values.
Results may differ from the reference program's by a relative error of at most 0.0096.
Values may be sent and summed in bfloat16 or wider, within the bound.
No kernel may reach another device: no remote copies, remote signals or barrier semaphores. Data moves between devices by JAX's collectives and lax.ppermute only.
A program may use at most 192 MiB of HBM per device.

```python
import math
import jax
import jax.numpy as jnp
from jax import lax

DK = 192
DV = 128
HQ = 8
DM = 2560
BLK = 64
TOPK = 16
W = 512
SUF_DEV = 512
GROUPS = 4
SIBLINGS = 4
SUF = 1024
PREFIX = 16384
QB_DEV = 8
QBLK = 16
BPD = 32
NCMP = 256
OWNERS = 8
CAP = 24


def draw_kv_rows(key, salt_value, lead_shape):
    subkey = jax.random.fold_in(key, salt_value)
    key_part, value_part = jax.random.split(subkey, 2)
    full_shape = lead_shape + (GROUPS,)
    key_rows = jnp.clip(jax.random.normal(key_part, full_shape + (DK,)), -4.0, 4.0)
    value_rows = jnp.clip(jax.random.normal(value_part, full_shape + (DV,)), -4.0, 4.0)
    return jnp.concatenate([key_rows, value_rows], axis=-1).astype(jnp.bfloat16)


def draw_prefix_kv(key, part):
    return draw_kv_rows(key, 11, (PREFIX,))


def draw_suffix_kv(key, part):
    return draw_kv_rows(key, 12, (SIBLINGS, SUF))


def draw_queries(key, part):
    full_shape = (SIBLINGS, SUF, GROUPS, HQ * DK)
    noise_key = jax.random.fold_in(jax.random.fold_in(key, 13), 0)
    values = 2.0 * jnp.clip(jax.random.normal(noise_key, full_shape), -4.0, 4.0)
    return values.astype(jnp.bfloat16)


def draw_selected(key, part):
    ctx_devices = QBLK // QB_DEV
    slot_total = QB_DEV * TOPK
    pool_total = OWNERS * CAP

    def single_draw(subkey):
        first_key, order_key, local_key = jax.random.split(subkey, 3)
        first_owner = jax.random.randint(first_key, (), 0, OWNERS)
        copy_index = jnp.arange(pool_total, dtype=jnp.int32)
        owner_all = copy_index // CAP
        order_scores = jax.random.permutation(order_key, pool_total).astype(jnp.int32)
        order_scores = jnp.where(owner_all == first_owner, copy_index % CAP - CAP, order_scores)
        sorted_pos = jnp.argsort(order_scores, stable=True)
        slot_owner = owner_all[sorted_pos[:slot_total]]
        owner_match = (slot_owner[:, None] == jnp.arange(OWNERS, dtype=jnp.int32)[None, :]).astype(jnp.int32)
        slot_rank = jnp.sum((jnp.cumsum(owner_match, axis=0) - 1) * owner_match, axis=1)
        local_perm = jax.vmap(lambda owner_key: jax.random.permutation(owner_key, BPD))(jax.random.split(local_key, OWNERS))
        slot_local = local_perm[slot_owner, slot_rank].astype(jnp.int32)
        return (slot_owner * BPD + slot_local).astype(jnp.int32).reshape(QB_DEV, TOPK)
    subkeys = jax.random.split(jax.random.fold_in(key, 14), SIBLINGS * ctx_devices * GROUPS)
    drawn = jax.vmap(single_draw)(subkeys)
    drawn = drawn.reshape(SIBLINGS, ctx_devices, GROUPS, QB_DEV, TOPK)
    return jnp.transpose(drawn, (0, 1, 3, 2, 4)).reshape(SIBLINGS, QBLK, GROUPS, TOPK)


def draw_lengths(key, part):
    base_key, perm_key = jax.random.split(jax.random.fold_in(key, 15))
    drawn = jax.random.randint(base_key, (SIBLINGS,), SUF // 8, SUF + 1)
    order_perm = jax.random.permutation(perm_key, SIBLINGS)
    drawn = drawn.at[order_perm[0]].set(SUF)
    drawn = drawn.at[order_perm[1]].set(SUF // 8)
    return drawn.astype(jnp.int32)


def steps_of(key, extent, shards, smallest, largest):
    def one(dim, blocks):
        steps = jax.random.uniform(jax.random.fold_in(jax.random.fold_in(key, 6), dim), (blocks,), jnp.float32, smallest / len(shards), largest / len(shards))
        return jnp.repeat(jnp.exp(steps), extent[dim] // blocks).reshape((-1,) + (1,) * (len(extent) - dim - 1))

    level = one(*shards[0])
    for cut in shards[1:]:
        level = level * one(*cut)
    return level


def scatter_about(stream_key, shape, deviation, limit, cuts=(), kind=jnp.bfloat16):
    values = jax.random.normal(stream_key, shape, jnp.float32) * deviation
    if len(cuts) > 0:
        values = steps_of(stream_key, shape, cuts, -0.22, 0.18) * values
    return jnp.clip(values, min=-limit, max=limit).astype(kind)


def setup_inputs(seed: int = 0) -> dict:
    splits = jax.random.split(jax.random.key(seed), 9)
    return {
        "queries": draw_queries(jax.random.fold_in(splits[8], 71), 0),
        "suffix_kv": draw_suffix_kv(jax.random.fold_in(splits[8], 71), 0),
        "prefix_kv": draw_prefix_kv(jax.random.fold_in(splits[8], 71), 0),
        "pooling": jnp.clip(jnp.exp(jax.random.uniform(splits[3], (2, BLK), jnp.float32, math.log(0.03), math.log(0.3))), 0.03, 0.3),
        "gate_logits": scatter_about(splits[4], (SIBLINGS, SUF, GROUPS, 3 * HQ), 1.5, 6.0, ((0, 4), (1, 2), (2, 4)), jnp.float32),
        "selected": draw_selected(jax.random.fold_in(splits[8], 71), 0),
        "lengths": draw_lengths(jax.random.fold_in(splits[8], 71), 0),
        "w_out": scatter_about(splits[7], (GROUPS * HQ * DV, DM), (HQ * DV // 4) ** -0.5, 0.375, ((0, 4),)),
    }


def softmax_parts(scores):
    row_max = jnp.max(scores, axis=-1, keepdims=True)
    weights = jnp.exp(scores - row_max)
    row_total = jnp.sum(weights, axis=-1, keepdims=True)
    rounded = lax.optimization_barrier(weights.astype(jnp.bfloat16))
    return rounded.astype(jnp.float32), row_total


def compress(group_kv, pooling):
    blocks = group_kv.reshape(-1, BLK, DK + DV).astype(jnp.float32)
    comp_keys = jnp.einsum("bjd,j->bd", blocks[:, :, :DK], pooling[0], precision=lax.Precision.HIGHEST)
    comp_values = jnp.einsum("bjd,j->bd", blocks[:, :, DK:], pooling[1], precision=lax.Precision.HIGHEST)
    return jnp.concatenate([comp_keys, comp_values], axis=-1).astype(jnp.bfloat16)


def reference(queries, suffix_kv, prefix_kv, pooling, gate_logits, selected, lengths, w_out):
    score_scale = DK ** -0.5
    window_reach = -(-W // SUF_DEV)
    group_prefix = jnp.moveaxis(prefix_kv, 1, 0)
    compressed = lax.map(lambda group_kv: compress(group_kv, pooling), group_prefix)
    prefix_blocks = group_prefix.reshape(GROUPS, NCMP, BLK, DK + DV)

    def one_sibling(sib_inputs):
        sib_queries, sib_kv, sib_gates, sib_selected, sib_length = sib_inputs

        def one_group(group_inputs):
            group_queries, group_kv, group_gates, group_selected, group_comp, group_blocks = group_inputs
            padded_kv = jnp.concatenate([jnp.zeros((window_reach * SUF_DEV, DK + DV), group_kv.dtype), group_kv], axis=0)
            comp_float = group_comp.astype(jnp.float32)

            def one_block(block_index):
                row_begin = block_index * SUF_DEV
                query_rows = lax.dynamic_slice_in_dim(group_queries, row_begin, SUF_DEV, 0)
                query_rows = query_rows.reshape(SUF_DEV, HQ, DK).astype(jnp.float32)
                scores = jnp.einsum("rhd,kd->rhk", query_rows, comp_float[:, :DK]) * score_scale
                weights, row_total = softmax_parts(scores)
                comp_out = jnp.einsum("rhk,kd->rhd", weights, comp_float[:, DK:]) / row_total

                block_ids = lax.dynamic_slice_in_dim(group_selected, block_index * QB_DEV, QB_DEV, 0)
                picked = group_blocks[block_ids].reshape(QB_DEV, TOPK * BLK, DK + DV).astype(jnp.float32)
                query_blocks = query_rows.reshape(QB_DEV, BLK, HQ, DK)
                scores = jnp.einsum("qthd,qkd->qhtk", query_blocks, picked[:, :, :DK]) * score_scale
                weights, row_total = softmax_parts(scores)
                sel_out = jnp.einsum("qhtk,qkd->qhtd", weights, picked[:, :, DK:]) / row_total
                sel_out = jnp.transpose(sel_out, (0, 2, 1, 3)).reshape(SUF_DEV, HQ, DV)

                near_kv = lax.dynamic_slice_in_dim(padded_kv, row_begin, (window_reach + 1) * SUF_DEV, 0).astype(jnp.float32)
                query_pos = row_begin + jnp.arange(SUF_DEV, dtype=jnp.int32)
                key_pos = row_begin - window_reach * SUF_DEV + jnp.arange((window_reach + 1) * SUF_DEV, dtype=jnp.int32)
                visible = (key_pos[None, :] <= query_pos[:, None]) & (key_pos[None, :] > query_pos[:, None] - W) & (key_pos[None, :] >= 0)
                scores = jnp.einsum("rhd,kd->rhk", query_rows, near_kv[:, :DK]) * score_scale
                scores = jnp.where(visible[:, None, :], scores, -jnp.inf)
                weights, row_total = softmax_parts(scores)
                win_out = jnp.einsum("rhk,kd->rhd", weights, near_kv[:, DK:]) / row_total

                gate_rows = lax.dynamic_slice_in_dim(group_gates, row_begin, SUF_DEV, 0)
                gate_values = jax.nn.sigmoid(gate_rows.reshape(SUF_DEV, 3, HQ))
                head_out = gate_values[:, 0, :, None] * comp_out + gate_values[:, 1, :, None] * sel_out + gate_values[:, 2, :, None] * win_out
                head_out = jnp.where((query_pos < sib_length)[:, None, None], head_out, 0.0)
                return head_out.astype(jnp.bfloat16).reshape(SUF_DEV, HQ * DV)

            block_outs = lax.map(one_block, jnp.arange(SUF // SUF_DEV, dtype=jnp.int32))
            return block_outs.reshape(SUF, HQ * DV)

        group_outs = lax.map(one_group, (jnp.moveaxis(sib_queries, 1, 0), jnp.moveaxis(sib_kv, 1, 0), jnp.moveaxis(sib_gates, 1, 0), jnp.moveaxis(sib_selected, 1, 0), compressed, prefix_blocks))
        joined = jnp.moveaxis(group_outs, 0, 1).reshape(SUF, GROUPS * HQ * DV)
        return jnp.dot(joined, w_out, preferred_element_type=jnp.float32).astype(jnp.bfloat16)

    return lax.map(one_sibling, (queries, suffix_kv, gate_logits, selected, lengths))
```

```python
import functools

import jax
import jax.numpy as jnp
from jax import lax
from jax.experimental import pallas as pl
from jax.experimental.pallas import tpu as pltpu
from jax.sharding import PartitionSpec as P

DK = 192
DV = 128
HQ = 8
DM = 2560
BLK = 64
W = 512
LANES = 128
TAIL = DK - LANES
EXT = 2 * LANES
ROWS = BLK + BLK // 2 + BLK
QUAD = 4
SCALE = DK ** (-0.5)
LOW = -1e30
VMEM = 56 * 1024 * 1024
BF = jnp.bfloat16
F32 = jnp.float32


def params(**more):
    return pltpu.CompilerParams(vmem_limit_bytes=VMEM, **more)


def cost(microseconds):
    return pl.CostEstimate(flops=int(microseconds * 1e9), bytes_accessed=0, transcendentals=0)


def lane_is_low(shape):
    return lax.broadcasted_iota(jnp.int32, shape, len(shape) - 1) < TAIL


def pack_kernel(kv_ref, pool_ref, packed_ref, comp_ref):
    tokens = kv_ref.shape[1]
    pool = pool_ref[...]
    pool_key = jnp.broadcast_to(pool[:, 0:1], (BLK, LANES))
    pool_value = jnp.broadcast_to(pool[:, 1:2], (BLK, LANES))
    half = BLK // 2
    pool_tail = jnp.where(lane_is_low((half, LANES)), pool_key[:half], pool_key[half:])
    rows = []
    for tile in range(tokens // LANES):
        part = kv_ref[:, tile * LANES : (tile + 1) * LANES].astype(F32)
        keys = part[:LANES].T
        ends = part[LANES:DK]
        ends = jnp.concatenate([ends, pltpu.roll(ends, LANES - half, 1)], axis=0).T
        values = part[DK:].T
        for sub in range(LANES // BLK):
            base = (tile * (LANES // BLK) + sub) * ROWS
            at = sub * BLK
            key, end, value = keys[at : at + BLK], ends[at : at + half], values[at : at + BLK]
            packed_ref[base : base + BLK] = key.astype(BF)
            packed_ref[base + BLK : base + BLK + half] = end.astype(BF)
            packed_ref[base + BLK + half : base + ROWS] = value.astype(BF)
            comp_key = jnp.sum(key * pool_key, axis=0, keepdims=True)
            comp_end = jnp.sum(end * pool_tail, axis=0, keepdims=True)
            comp_end = comp_end + pltpu.roll(comp_end, TAIL, 1)
            comp_end = jnp.where(lane_is_low((1, LANES)), comp_end, 0.0)
            comp_value = jnp.sum(value * pool_value, axis=0, keepdims=True)
            rows.append(jnp.concatenate([comp_key, comp_end, comp_value], axis=1))
    comp_ref[...] = jnp.concatenate(rows, axis=0).astype(BF)


def pack(kv_t, pooling):
    blocks = kv_t.shape[1] // BLK
    return pl.pallas_call(
        pack_kernel,
        out_shape=(
            jax.ShapeDtypeStruct((blocks * ROWS, LANES), BF),
            jax.ShapeDtypeStruct((blocks, EXT + DV), BF),
        ),
        compiler_params=params(),
        cost_estimate=cost(5),
        name="pack",
    )(kv_t, pooling.T)


def wide_queries_kernel(q_ref, out_ref):
    low = lane_is_low((BLK, LANES))
    for pair in range(HQ // 2):
        at = pair * 2 * DK
        first, middle, last = (
            q_ref[:, at + k * LANES : at + (k + 1) * LANES].astype(F32) for k in range(3)
        )
        middle_swap = pltpu.roll(middle, TAIL, 1)
        last_swap = pltpu.roll(last, TAIL, 1)
        top = pair * 2 * BLK
        out_ref[0, top : top + BLK, :LANES] = first.astype(BF)
        out_ref[0, top : top + BLK, LANES:] = jnp.where(low, middle, middle_swap).astype(BF)
        top += BLK
        out_ref[0, top : top + BLK, :LANES] = jnp.where(low, middle_swap, last_swap).astype(BF)
        out_ref[0, top : top + BLK, LANES:] = jnp.where(low, last_swap, last).astype(BF)


def wide_queries(queries):
    rows = queries.shape[0]
    return pl.pallas_call(
        wide_queries_kernel,
        grid=(rows // BLK,),
        in_specs=[pl.BlockSpec((BLK, HQ * DK), lambda i: (i, 0))],
        out_specs=pl.BlockSpec((1, HQ * BLK, EXT), lambda i: (i, 0, 0)),
        out_shape=jax.ShapeDtypeStruct((rows // BLK, HQ * BLK, EXT), BF),
        compiler_params=params(),
        cost_estimate=cost(6),
        name="wide_queries",
    )(queries)


def scores_of(keys, queries):
    return lax.dot_general(keys, queries, (((1,), (1,)), ((), ())), preferred_element_type=F32)


def near_kernel(begin_ref, q_ref, far_ref, own_ref, comp_ref, gate_ref, out_ref, key_ref, value_ref):
    step = pl.program_id(0)
    rows = own_ref.shape[1]

    @pl.when(step == 0)
    def _():
        zeros = jnp.zeros((LANES, TAIL), BF)
        for source, top in ((far_ref, 0), (own_ref, rows)):
            for at in range(0, rows, LANES):
                part = source[:DK, at : at + LANES].astype(F32)
                key_ref[top + at : top + at + LANES, :LANES] = part[:LANES].T.astype(BF)
                end = jnp.concatenate([part[LANES:], jnp.zeros((TAIL, LANES), F32)], axis=0)
                key_ref[top + at : top + at + LANES, LANES:] = end.T.astype(BF)
            value_ref[:, top : top + rows] = source[DK:, :]

    queries = q_ref[0]
    gates = gate_ref[0]
    total_lanes = queries.shape[0]
    scores = scores_of(comp_ref[:, :EXT], queries)
    top = jnp.max(scores, axis=0, keepdims=True)
    weights = jnp.exp((scores - top) * SCALE)
    total = jnp.sum(weights, axis=0, keepdims=True)
    comp_out = lax.dot_general(
        comp_ref[:, EXT:], weights.astype(BF), (((0,), (0,)), ((), ())), preferred_element_type=F32
    )
    out = comp_out * (gates[0:1] / total)

    span = W + LANES
    start = pl.multiple_of((step // 2) * LANES + rows - W, LANES)
    scores = scores_of(key_ref[pl.ds(start, span), :], queries)
    key_pos = start - rows + lax.broadcasted_iota(jnp.int32, (span, total_lanes), 0)
    query_pos = step * BLK + (lax.broadcasted_iota(jnp.int32, (span, total_lanes), 1) & (BLK - 1))
    visible = (key_pos <= query_pos) & (key_pos > query_pos - W) & (key_pos + begin_ref[0] >= 0)
    scores = jnp.where(visible, scores, LOW)
    top = jnp.max(scores, axis=0, keepdims=True)
    weights = jnp.exp((scores - top) * SCALE)
    total = jnp.sum(weights, axis=0, keepdims=True)
    window_out = jnp.dot(
        value_ref[:, pl.ds(start, span)], weights.astype(BF), preferred_element_type=F32
    )
    out_ref[0] = out + window_out * (gates[2:3] / total)


def near_parts(begin, wide, far_t, own_t, comp, gates):
    steps, lanes, _ = wide.shape
    rows = own_t.shape[1]
    whole = lambda array: pl.BlockSpec(array.shape, lambda i, *_: (0,) * array.ndim)
    return pl.pallas_call(
        near_kernel,
        grid_spec=pltpu.PrefetchScalarGridSpec(
            num_scalar_prefetch=1,
            grid=(steps,),
            in_specs=[
                pl.BlockSpec((1, lanes, EXT), lambda i, *_: (i, 0, 0)),
                whole(far_t),
                whole(own_t),
                whole(comp),
                pl.BlockSpec((1, 3, lanes), lambda i, *_: (i, 0, 0)),
            ],
            out_specs=pl.BlockSpec((1, DV, lanes), lambda i, *_: (i, 0, 0)),
            scratch_shapes=[pltpu.VMEM((2 * rows, EXT), BF), pltpu.VMEM((DV, 2 * rows), BF)],
        ),
        out_shape=jax.ShapeDtypeStruct((steps, DV, lanes), F32),
        compiler_params=params(),
        cost_estimate=cost(14),
        name="near",
    )(begin, wide, far_t, own_t, comp, gates)


def selected_step(block, ids_ref, owner_ref, q_ref, kv_refs, state, list_ref, key_ref, value_ref):
    top_k = ids_ref.shape[1]
    held = kv_refs[0].shape[0] // ROWS
    count = jnp.int32(0)
    for slot in range(top_k):
        index = ids_ref[block, slot]
        owner = index // held
        entry = jnp.int32(-1)
        for place in range(len(kv_refs)):
            entry = jnp.where(owner == owner_ref[place], place * held + index % held, entry)
        list_ref[count] = entry
        count = count + (entry >= 0).astype(jnp.int32)
    half = BLK // 2
    low = lane_is_low((half, LANES))

    def quad(step, state):
        top, total, acc = state
        for k in range(QUAD):
            entry = list_ref[jnp.minimum(step * QUAD + k, count - 1)]
            place, base = entry // held, pl.multiple_of((entry % held) * ROWS, 16)
            for at, kv_ref in enumerate(kv_refs):

                @pl.when(place == at)
                def _():
                    to = k * BLK
                    key_ref[to : to + BLK, :LANES] = kv_ref[pl.ds(base, BLK), :]
                    end = kv_ref[pl.ds(base + BLK, half), :]
                    zero = jnp.zeros_like(end)
                    key_ref[to : to + half, LANES:] = jnp.where(low, end, zero)
                    key_ref[to + half : to + BLK, LANES:] = jnp.where(low, zero, end)
                    value_ref[to : to + BLK, :] = kv_ref[pl.ds(base + BLK + half, BLK), :]

        scores = scores_of(key_ref[...], q_ref[0])
        row = lax.broadcasted_iota(jnp.int32, scores.shape, 0)
        scores = jnp.where(row < (count - step * QUAD) * BLK, scores, LOW)
        new_top = jnp.maximum(top, jnp.max(scores, axis=0, keepdims=True))
        weights = jnp.exp((scores - new_top) * SCALE)
        keep = jnp.exp((top - new_top) * SCALE)
        total = total * keep + jnp.sum(weights, axis=0, keepdims=True)
        acc = acc * keep + lax.dot_general(
            value_ref[...], weights.astype(BF), (((0,), (0,)), ((), ())), preferred_element_type=F32
        )
        return new_top, total, acc

    return lax.fori_loop(0, (count + QUAD - 1) // QUAD, quad, state)


def stage_kernel(first, n_kv, ids_ref, owner_ref, q_ref, *refs):
    kv_refs, refs = refs[:n_kv], refs[n_kv:]
    if first:
        state_out, acc_out, list_ref, key_ref, value_ref = refs
        lanes = q_ref.shape[1]
        state = (
            jnp.full((1, lanes), LOW, F32),
            jnp.zeros((1, lanes), F32),
            jnp.zeros((DV, lanes), F32),
        )
    else:
        state_in, acc_in, state_out, acc_out, list_ref, key_ref, value_ref = refs
        state = (state_in[0, 0:1], state_in[0, 1:2], acc_in[0])
    top, total, acc = selected_step(
        pl.program_id(0), ids_ref, owner_ref, q_ref, kv_refs, state, list_ref, key_ref, value_ref
    )
    state_out[0, 0:1] = top
    state_out[0, 1:2] = total
    acc_out[0] = acc


def scratch():
    return [
        pltpu.SMEM((64,), jnp.int32),
        pltpu.VMEM((QUAD * BLK, EXT), BF),
        pltpu.VMEM((QUAD * BLK, DV), BF),
    ]


def stage(ids, owners, wide, kvs, state):
    steps, lanes, _ = wide.shape
    row = pl.BlockSpec((1, 2, lanes), lambda i, *_: (i, 0, 0))
    wide_row = pl.BlockSpec((1, DV, lanes), lambda i, *_: (i, 0, 0))
    in_specs = [pl.BlockSpec((1, lanes, EXT), lambda i, *_: (i, 0, 0))]
    in_specs += [pl.BlockSpec(kv.shape, lambda i, *_: (0, 0)) for kv in kvs]
    first = state is None
    aliases = {}
    if not first:
        in_specs += [row, wide_row]
        aliases = {3 + len(kvs): 0, 4 + len(kvs): 1}
    return pl.pallas_call(
        functools.partial(stage_kernel, first, len(kvs)),
        grid_spec=pltpu.PrefetchScalarGridSpec(
            num_scalar_prefetch=2,
            grid=(steps,),
            in_specs=in_specs,
            out_specs=[row, wide_row],
            scratch_shapes=scratch(),
        ),
        out_shape=(
            jax.ShapeDtypeStruct((steps, 2, lanes), F32),
            jax.ShapeDtypeStruct((steps, DV, lanes), F32),
        ),
        input_output_aliases=aliases,
        compiler_params=params(),
        cost_estimate=cost(12),
        name="stage",
    )(ids, owners, wide, *kvs, *(() if first else state))


def last_kernel(n_kv, order_ref, ids_ref, owner_ref, q_ref, *refs):
    kv_refs, refs = refs[:n_kv], refs[n_kv:]
    state_in, acc_in, near_ref, gate_ref, out_ref, list_ref, key_ref, value_ref = refs
    state = (state_in[0, 0:1], state_in[0, 1:2], acc_in[0])
    block = order_ref[pl.program_id(0)]
    _, total, acc = selected_step(
        block, ids_ref, owner_ref, q_ref, kv_refs, state, list_ref, key_ref, value_ref
    )
    out = near_ref[0] + acc * (gate_ref[0, 1:2] / total)
    for head in range(0, HQ, 2):
        pair = out[:, head * BLK : (head + 2) * BLK].T.astype(BF)
        out_ref[:, head * DV : (head + 1) * DV] = pair[:BLK]
        out_ref[:, (head + 1) * DV : (head + 2) * DV] = pair[BLK:]


def last_stage(order, ids, owners, wide, kvs, state, near, gates):
    _, lanes, _ = wide.shape
    (steps,) = order.shape
    at = lambda i, order, *_: (order[i], 0, 0)
    return pl.pallas_call(
        functools.partial(last_kernel, len(kvs)),
        grid_spec=pltpu.PrefetchScalarGridSpec(
            num_scalar_prefetch=3,
            grid=(steps,),
            in_specs=[pl.BlockSpec((1, lanes, EXT), at)]
            + [pl.BlockSpec(kv.shape, lambda i, *_: (0, 0)) for kv in kvs]
            + [
                pl.BlockSpec((1, 2, lanes), at),
                pl.BlockSpec((1, DV, lanes), at),
                pl.BlockSpec((1, DV, lanes), at),
                pl.BlockSpec((1, 3, lanes), at),
            ],
            out_specs=pl.BlockSpec((BLK, HQ * DV), lambda i, *_: (i, 0)),
            scratch_shapes=scratch(),
        ),
        out_shape=jax.ShapeDtypeStruct((steps * BLK, HQ * DV), BF),
        compiler_params=params(),
        cost_estimate=cost(8),
        name="last_stage",
    )(order, ids, owners, wide, *kvs, *state, near, gates)


def swap(value, axis, bit):
    return lax.ppermute(value, axis, [(i, i ^ bit) for i in range(lax.axis_size(axis))])


def spread(value, axis, wraps, sib_shift):
    sib_count, count = lax.axis_size("sib"), lax.axis_size(axis)
    ring = wraps or count == 2
    reach = [count // 2, (count - 1) // 2] if ring else [count - 1, count - 1]
    held = [value, value]
    found = []
    for hop in range(1, max(reach) + 1):
        for side, sign in enumerate((1, -1)):
            if hop > reach[side]:
                continue
            pairs = []
            for source in range(count):
                target = source + sign
                if ring:
                    pairs.append((source, target % count))
                elif 0 <= target < count and 0 <= target - sign * hop < count:
                    pairs.append((source, target))
            axes = axis
            if axis == "ctx":
                axes = ("sib", "ctx")
                holders = [s for s in range(sib_count) if wraps or 0 <= s + sib_shift < sib_count]
                pairs = [(s * count + a, s * count + b) for s in holders for a, b in pairs]
            held[side] = lax.ppermute(held[side], axes, pairs)
            found.append((held[side], hop, -sign * hop))
    return found


def shards(wraps, queries, suffix_kv, prefix_kv, pooling, gate_logits, selected, lengths, w_out):
    rows = queries.shape[1]
    sib_count, ctx_count, head_count = (lax.axis_size(a) for a in ("sib", "ctx", "head"))
    blocks = rows // BLK
    sib, ctx, head = (lax.axis_index(a) for a in ("sib", "ctx", "head"))
    packed, comp = pack(prefix_kv[:, 0, :].T, pooling)

    own_t = suffix_kv[0, :, 0, :].T
    far_t = lax.ppermute(own_t, "ctx", [(i, i + 1) for i in range(ctx_count - 1)])
    for axis, count in (("ctx", ctx_count), ("sib", sib_count)):
        bit = 1
        while bit < count:
            comp = jnp.concatenate([comp, swap(comp, axis, bit)], axis=0)
            bit *= 2

    def owner_of(sib_shift, ctx_shift):
        s, c = sib + sib_shift, ctx + ctx_shift
        if wraps:
            s = s % sib_count
        if wraps or ctx_count == 2:
            c = c % ctx_count
        good = (s >= 0) & (s < sib_count) & (c >= 0) & (c < ctx_count)
        return jnp.where(good, s * ctx_count + c, -2)

    levels = {0: [(packed, 0)]}
    for array, hop, shift in spread(packed, "sib", wraps, 0):
        levels.setdefault(hop, []).append((array, shift))
    stages = []
    for hop, arrivals in levels.items():
        near_by, far_off = [], []
        for array, shift in arrivals:
            near_by.append((array, owner_of(shift, 0)))
            for other, _, ctx_shift in spread(array, "ctx", wraps, shift):
                far_off.append((other, owner_of(shift, ctx_shift)))
        stages.append((near_by, far_off))

    wide = wide_queries(queries.reshape(rows, HQ * DK))
    begin = (ctx * rows).astype(jnp.int32)
    gates = jax.nn.sigmoid(gate_logits.reshape(rows, 3, HQ))
    alive = begin + jnp.arange(rows, dtype=jnp.int32) < lengths[0]
    gates = jnp.where(alive[:, None, None], gates, 0.0)
    gates = gates.reshape(blocks, BLK, 3, HQ).transpose(0, 2, 3, 1).reshape(blocks, 3, HQ * BLK)
    near = near_parts(begin.reshape(1), wide, far_t, own_t, comp, gates)

    ids = selected.reshape(blocks, -1)
    work = []
    for near_by, far_off in stages[:-1]:
        work.append(near_by + far_off)
    work.append(stages[-1][0])
    state = None
    for items in work:
        owners = jnp.stack([o for _, o in items]).astype(jnp.int32)
        state = stage(ids, owners, wide, [a for a, _ in items], state)
    items = stages[-1][1]
    owners = jnp.stack([o for _, o in items]).astype(jnp.int32)
    kvs = [a for a, _ in items]

    half = head_count // 2
    chunk = rows // head_count
    per = chunk // BLK
    high, low = head // half, head % half

    def half_order(which):
        starts = [(which * half + (low ^ k)) * per for k in range(half - 1, -1, -1)]
        return jnp.concatenate([s + jnp.arange(per, dtype=jnp.int32) for s in starts])

    def half_sum(which):
        out = last_stage(half_order(which), ids, owners, wide, kvs, state, near, gates)
        share = jnp.dot(out, w_out, preferred_element_type=F32)
        other = swap(share[:chunk].astype(BF), "head", 1)
        return share[chunk:] + other.astype(F32)

    away = half_sum(1 - high)
    back = swap(away.astype(BF), "head", half)
    mine = half_sum(high)
    return (mine + back.astype(F32)).astype(BF).reshape(1, chunk, DM)


def solution(mesh):
    wraps = mesh.size >= 128
    return jax.shard_map(
        functools.partial(shards, wraps),
        mesh=mesh,
        in_specs=(
            P("sib", "ctx", "head", None),
            P("sib", "ctx", "head", None),
            P(("sib", "ctx"), "head", None),
            P(),
            P("sib", "ctx", "head", None),
            P("sib", "ctx", "head", None),
            P("sib"),
            P("head", None),
        ),
        out_specs=P("sib", ("ctx", "head"), None),
        check_vma=False,
    )
```

```python
import functools

import jax
import jax.numpy as jnp
from jax import lax
from jax.experimental import pallas as pl
from jax.experimental.pallas import tpu as pltpu
from jax.sharding import PartitionSpec as P

DK = 192
DV = 128
HQ = 8
DM = 2560
BLK = 64
W = 512
LANES = 128
TAIL = DK - LANES
EXT = 2 * LANES
ROWS = BLK + BLK // 2 + BLK
UNIT = 4
NOTES = 16
PIECES = 2
SCALE = DK ** (-0.5)
LOW = -1e30
VMEM = 32 * 1024 * 1024
BF = jnp.bfloat16
F32 = jnp.float32


def params(**more):
    return pltpu.CompilerParams(vmem_limit_bytes=VMEM, **more)


def cost(microseconds):
    return pl.CostEstimate(flops=int(microseconds * 1e9), bytes_accessed=0, transcendentals=0)


def lane_is_low(shape):
    return lax.broadcasted_iota(jnp.int32, shape, len(shape) - 1) < TAIL


def pack_kernel(kv_ref, pool_ref, packed_ref, comp_ref):
    tokens = kv_ref.shape[1]
    pool_key, pool_value = (
        jnp.broadcast_to(pool_ref[k : k + 1, :], (LANES, BLK)).T for k in range(2)
    )
    half = BLK // 2
    pool_tail = jnp.where(lane_is_low((half, LANES)), pool_key[:half], pool_key[half:])
    rows = []
    for tile in range(tokens // LANES):
        part = kv_ref[:, tile * LANES : (tile + 1) * LANES].astype(F32)
        keys = part[:LANES].T
        ends = part[LANES:DK]
        ends = jnp.concatenate([ends, pltpu.roll(ends, LANES - half, 1)], axis=0).T
        values = part[DK:].T
        for sub in range(LANES // BLK):
            base = (tile * (LANES // BLK) + sub) * ROWS
            at = sub * BLK
            key, end, value = keys[at : at + BLK], ends[at : at + half], values[at : at + BLK]
            packed_ref[base : base + BLK] = key.astype(BF)
            packed_ref[base + BLK : base + BLK + half] = end.astype(BF)
            packed_ref[base + BLK + half : base + ROWS] = value.astype(BF)
            comp_key = jnp.sum(key * pool_key, axis=0, keepdims=True)
            comp_end = jnp.sum(end * pool_tail, axis=0, keepdims=True)
            comp_end = comp_end + pltpu.roll(comp_end, TAIL, 1)
            comp_end = jnp.where(lane_is_low((1, LANES)), comp_end, 0.0)
            comp_value = jnp.sum(value * pool_value, axis=0, keepdims=True)
            rows.append(jnp.concatenate([comp_key, comp_end, comp_value], axis=1))
    comp_ref[...] = jnp.concatenate(rows, axis=0).astype(BF)


def pack(kv_t, pooling):
    blocks = kv_t.shape[1] // BLK
    return pl.pallas_call(
        pack_kernel,
        out_shape=(
            jax.ShapeDtypeStruct((blocks * ROWS, LANES), BF),
            jax.ShapeDtypeStruct((blocks, EXT + DV), BF),
        ),
        compiler_params=params(),
        cost_estimate=cost(5),
        name="pack",
    )(kv_t, pooling)


def wide_queries_kernel(q_ref, out_ref):
    low = lane_is_low((BLK, LANES))
    for pair in range(HQ // 2):
        at = pair * 2 * DK
        first, middle, last = (
            q_ref[:, at + k * LANES : at + (k + 1) * LANES].astype(F32) for k in range(3)
        )
        middle_swap = pltpu.roll(middle, TAIL, 1)
        last_swap = pltpu.roll(last, TAIL, 1)
        top = pair * 2 * BLK
        out_ref[0, top : top + BLK, :LANES] = first.astype(BF)
        out_ref[0, top : top + BLK, LANES:] = jnp.where(low, middle, middle_swap).astype(BF)
        top += BLK
        out_ref[0, top : top + BLK, :LANES] = jnp.where(low, middle_swap, last_swap).astype(BF)
        out_ref[0, top : top + BLK, LANES:] = jnp.where(low, last_swap, last).astype(BF)


def wide_queries(queries):
    rows = queries.shape[0]
    return pl.pallas_call(
        wide_queries_kernel,
        grid=(rows // BLK,),
        in_specs=[pl.BlockSpec((BLK, HQ * DK), lambda i: (i, 0))],
        out_specs=pl.BlockSpec((1, HQ * BLK, EXT), lambda i: (i, 0, 0)),
        out_shape=jax.ShapeDtypeStruct((rows // BLK, HQ * BLK, EXT), BF),
        compiler_params=params(),
        cost_estimate=cost(6),
        name="wide_queries",
    )(queries)


def scores_of(keys, queries):
    return lax.dot_general(keys, queries, (((1,), (1,)), ((), ())), preferred_element_type=F32)


def near_kernel(begin_ref, q_ref, far_ref, own_ref, comp_ref, gate_ref, out_ref, key_ref, value_ref):
    step = pl.program_id(0)
    rows = own_ref.shape[1]

    @pl.when(step == 0)
    def _():
        zeros = jnp.zeros((LANES, TAIL), BF)
        for source, top in ((far_ref, 0), (own_ref, rows)):
            for at in range(0, rows, LANES):
                part = source[:DK, at : at + LANES].astype(F32)
                key_ref[top + at : top + at + LANES, :LANES] = part[:LANES].T.astype(BF)
                end = jnp.concatenate([part[LANES:], jnp.zeros((TAIL, LANES), F32)], axis=0)
                key_ref[top + at : top + at + LANES, LANES:] = end.T.astype(BF)
            value_ref[:, top : top + rows] = source[DK:, :]

    queries = q_ref[0]
    gates = gate_ref[0]
    total_lanes = queries.shape[0]
    scores = scores_of(comp_ref[:, :EXT], queries)
    top = jnp.max(scores, axis=0, keepdims=True)
    weights = jnp.exp((scores - top) * SCALE)
    total = jnp.sum(weights, axis=0, keepdims=True)
    comp_out = lax.dot_general(
        comp_ref[:, EXT:], weights.astype(BF), (((0,), (0,)), ((), ())), preferred_element_type=F32
    )
    out = comp_out * (gates[0:1] / total)

    span = W + LANES
    start = pl.multiple_of((step // 2) * LANES + rows - W, LANES)
    scores = scores_of(key_ref[pl.ds(start, span), :], queries)
    key_pos = start - rows + lax.broadcasted_iota(jnp.int32, (span, total_lanes), 0)
    query_pos = step * BLK + (lax.broadcasted_iota(jnp.int32, (span, total_lanes), 1) & (BLK - 1))
    visible = (key_pos <= query_pos) & (key_pos > query_pos - W) & (key_pos + begin_ref[0] >= 0)
    scores = jnp.where(visible, scores, LOW)
    top = jnp.max(scores, axis=0, keepdims=True)
    weights = jnp.exp((scores - top) * SCALE)
    total = jnp.sum(weights, axis=0, keepdims=True)
    window_out = jnp.dot(
        value_ref[:, pl.ds(start, span)], weights.astype(BF), preferred_element_type=F32
    )
    out_ref[0] = out + window_out * (gates[2:3] / total)


def near_parts(begin, wide, far_t, own_t, comp, gates):
    steps, lanes, _ = wide.shape
    rows = own_t.shape[1]
    whole = lambda array: pl.BlockSpec(array.shape, lambda i, *_: (0,) * array.ndim)
    return pl.pallas_call(
        near_kernel,
        grid_spec=pltpu.PrefetchScalarGridSpec(
            num_scalar_prefetch=1,
            grid=(steps,),
            in_specs=[
                pl.BlockSpec((1, lanes, EXT), lambda i, *_: (i, 0, 0)),
                whole(far_t),
                whole(own_t),
                whole(comp),
                pl.BlockSpec((1, 3, lanes), lambda i, *_: (i, 0, 0)),
            ],
            out_specs=pl.BlockSpec((1, DV, lanes), lambda i, *_: (i, 0, 0)),
            scratch_shapes=[pltpu.VMEM((2 * rows, EXT), BF), pltpu.VMEM((DV, 2 * rows), BF)],
        ),
        out_shape=jax.ShapeDtypeStruct((steps, DV, lanes), F32),
        compiler_params=params(),
        cost_estimate=cost(14),
        name="near",
    )(begin, wide, far_t, own_t, comp, gates)


def add_selected(unit, list_ref, block, q_ref, kv_refs, top, total, acc_ref, key_ref, value_ref):
    count = list_ref[block, list_ref.shape[1] - 1]
    held = kv_refs[0].shape[0]
    half = BLK // 2
    low = lane_is_low((half, LANES))

    def step(index, state):
        top, total = state
        for k in range(unit):
            entry = list_ref[block, jnp.minimum(index * unit + k, count - 1)]
            for place, kv_ref in enumerate(kv_refs):
                inside = (entry >= place * held) & (entry < (place + 1) * held)

                @pl.when(inside)
                def _(kv_ref=kv_ref, place=place):
                    base = pl.multiple_of(entry - place * held, 32)
                    to = k * BLK
                    key_ref[to : to + BLK, :LANES] = kv_ref[pl.ds(base, BLK), :]
                    end = kv_ref[pl.ds(base + BLK, half), :]
                    zero = jnp.zeros_like(end)
                    key_ref[to : to + half, LANES:] = jnp.where(low, end, zero)
                    key_ref[to + half : to + BLK, LANES:] = jnp.where(low, zero, end)
                    value_ref[to : to + BLK, :] = kv_ref[pl.ds(base + BLK + half, BLK), :]

        keys = unit * BLK
        scores = scores_of(key_ref[:keys], q_ref[0])
        row = lax.broadcasted_iota(jnp.int32, scores.shape, 0)
        scores = jnp.where(row < (count - index * unit) * BLK, scores, LOW)
        new_top = jnp.maximum(top, jnp.max(scores, axis=0, keepdims=True))
        weights = jnp.exp((scores - new_top) * SCALE)
        keep = jnp.exp((top - new_top) * SCALE)
        total = total * keep + jnp.sum(weights, axis=0, keepdims=True)
        acc_ref[...] = acc_ref[...] * keep + lax.dot_general(
            value_ref[:keys],
            weights.astype(BF),
            (((0,), (0,)), ((), ())),
            preferred_element_type=F32,
        )
        return new_top, total

    return lax.fori_loop(0, (count + unit - 1) // unit, step, (top, total))


def scratch(unit):
    return [pltpu.VMEM((unit * BLK, EXT), BF), pltpu.VMEM((unit * BLK, DV), BF)]


def whole_spec(array):
    return pl.BlockSpec(array.shape, lambda i, *_: (0,) * array.ndim)


def stage_kernel(first, n_kv, unit, list_ref, q_ref, *refs):
    kv_refs, refs = refs[:n_kv], refs[n_kv:]
    lanes = q_ref.shape[1]
    if first:
        state_out, acc_out, key_ref, value_ref = refs
        top = jnp.full((1, lanes), LOW, F32)
        total = jnp.zeros((1, lanes), F32)
        acc_out[...] = jnp.zeros_like(acc_out)
    else:
        state_in, acc_in, state_out, acc_out, key_ref, value_ref = refs
        top, total = state_in[0, 0:1], state_in[0, 1:2]
        acc_out[...] = acc_in[...]
    top, total = add_selected(
        unit, list_ref, pl.program_id(0), q_ref, kv_refs, top, total, acc_out.at[0], key_ref, value_ref
    )
    state_out[0, 0:1] = top
    state_out[0, 1:2] = total


def stage(unit, lists, wide, kvs, state):
    steps, lanes, _ = wide.shape
    row = pl.BlockSpec((1, 2, lanes), lambda i, *_: (i, 0, 0))
    wide_row = pl.BlockSpec((1, DV, lanes), lambda i, *_: (i, 0, 0))
    in_specs = [pl.BlockSpec((1, lanes, EXT), lambda i, *_: (i, 0, 0))]
    in_specs += [whole_spec(kv) for kv in kvs]
    first = state is None
    aliases = {}
    if not first:
        in_specs += [row, wide_row]
        aliases = {2 + len(kvs): 0, 3 + len(kvs): 1}
    return pl.pallas_call(
        functools.partial(stage_kernel, first, len(kvs), unit),
        grid_spec=pltpu.PrefetchScalarGridSpec(
            num_scalar_prefetch=1,
            grid=(steps,),
            in_specs=in_specs,
            out_specs=[row, wide_row],
            scratch_shapes=scratch(unit),
        ),
        out_shape=(
            jax.ShapeDtypeStruct((steps, 2, lanes), F32),
            jax.ShapeDtypeStruct((steps, DV, lanes), F32),
        ),
        input_output_aliases=aliases,
        compiler_params=params(),
        cost_estimate=cost(9),
        name="stage",
    )(lists, wide, *kvs, *(() if first else state))


def log_total(top, total):
    return jnp.where(total > 0, top * SCALE + jnp.log(jnp.maximum(total, 1e-30)), LOW)


def part_kernel(n_kv, unit, order_ref, list_ref, q_ref, *refs):
    kv_refs, refs = refs[:n_kv], refs[n_kv:]
    state_in, acc_in, out_ref, acc_ref, key_ref, value_ref = refs
    acc_ref[...] = acc_in[0]
    top, total = add_selected(
        unit,
        list_ref,
        order_ref[pl.program_id(0)],
        q_ref,
        kv_refs,
        state_in[0, 0:1],
        state_in[0, 1:2],
        acc_ref,
        key_ref,
        value_ref,
    )
    out_ref[0, :DV] = (acc_ref[...] / jnp.maximum(total, 1e-30)).astype(BF)
    rest = log_total(top, total)
    terms = []
    for _ in range(3):
        terms.append(rest.astype(BF).astype(F32))
        rest = rest - terms[-1]
    terms.append(jnp.zeros((NOTES - len(terms), rest.shape[1]), F32))
    out_ref[0, DV:] = jnp.concatenate(terms, axis=0).astype(BF)


def part_stage(unit, order, lists, wide, kvs, state):
    _, lanes, _ = wide.shape
    (steps,) = order.shape
    at = lambda i, order, *_: (order[i], 0, 0)
    return pl.pallas_call(
        functools.partial(part_kernel, len(kvs), unit),
        grid_spec=pltpu.PrefetchScalarGridSpec(
            num_scalar_prefetch=2,
            grid=(steps,),
            in_specs=[pl.BlockSpec((1, lanes, EXT), at)]
            + [whole_spec(kv) for kv in kvs]
            + [pl.BlockSpec((1, 2, lanes), at), pl.BlockSpec((1, DV, lanes), at)],
            out_specs=pl.BlockSpec((1, DV + NOTES, lanes), lambda i, *_: (i, 0, 0)),
            scratch_shapes=[pltpu.VMEM((DV, lanes), F32)] + scratch(unit),
        ),
        out_shape=jax.ShapeDtypeStruct((steps, DV + NOTES, lanes), BF),
        compiler_params=params(),
        cost_estimate=cost(4),
        name="part_stage",
    )(order, lists, wide, *kvs, *state)


def last_kernel(n_kv, unit, order_ref, list_ref, q_ref, *refs):
    kv_refs, refs = refs[:n_kv], refs[n_kv:]
    state_in, acc_in, near_ref, gate_ref = refs[:4]
    part_refs, (out_ref, acc_ref, key_ref, value_ref) = refs[4:-4], refs[-4:]
    acc_ref[...] = acc_in[0]
    top, total = add_selected(
        unit,
        list_ref,
        order_ref[pl.program_id(0)],
        q_ref,
        kv_refs,
        state_in[0, 0:1],
        state_in[0, 1:2],
        acc_ref,
        key_ref,
        value_ref,
    )
    logs = [log_total(top, total)]
    for part_ref in part_refs:
        notes = part_ref[0, DV:].astype(F32)
        logs.append(notes[0:1] + notes[1:2] + notes[2:3])
    peak = functools.reduce(jnp.maximum, logs)
    shares = [jnp.exp(log - peak) for log in logs]
    gate = gate_ref[0, 1:2] / functools.reduce(jnp.add, shares)
    out = near_ref[0] + acc_ref[...] * (gate * shares[0] / jnp.maximum(total, 1e-30))
    for share, part_ref in zip(shares[1:], part_refs):
        out = out + part_ref[0, :DV].astype(F32) * (gate * share)
    for head in range(0, HQ, 2):
        pair = out[:, head * BLK : (head + 2) * BLK].T.astype(BF)
        out_ref[:, head * DV : (head + 1) * DV] = pair[:BLK]
        out_ref[:, (head + 1) * DV : (head + 2) * DV] = pair[BLK:]


def last_stage(unit, order, lists, wide, kvs, state, near, gates, others):
    _, lanes, _ = wide.shape
    (steps,) = order.shape
    at = lambda i, order, *_: (order[i], 0, 0)
    return pl.pallas_call(
        functools.partial(last_kernel, len(kvs), unit),
        grid_spec=pltpu.PrefetchScalarGridSpec(
            num_scalar_prefetch=2,
            grid=(steps,),
            in_specs=[pl.BlockSpec((1, lanes, EXT), at)]
            + [whole_spec(kv) for kv in kvs]
            + [
                pl.BlockSpec((1, 2, lanes), at),
                pl.BlockSpec((1, DV, lanes), at),
                pl.BlockSpec((1, DV, lanes), at),
                pl.BlockSpec((1, 3, lanes), at),
            ]
            + [pl.BlockSpec((1, DV + NOTES, lanes), lambda i, *_: (i, 0, 0)) for _ in others],
            out_specs=pl.BlockSpec((BLK, HQ * DV), lambda i, *_: (i, 0)),
            scratch_shapes=[pltpu.VMEM((DV, lanes), F32)] + scratch(unit),
        ),
        out_shape=jax.ShapeDtypeStruct((steps * BLK, HQ * DV), BF),
        compiler_params=params(),
        cost_estimate=cost(5),
        name="last_stage",
    )(order, lists, wide, *kvs, *state, near, gates, *others)


def held_lists(ids, owners, held):
    top_k = ids.shape[-1]
    owner = ids // held
    entry = (ids % held) * ROWS
    match = jnp.zeros(ids.shape, jnp.bool_)
    for place, one in enumerate(owners):
        here = owner == one
        match = match | here
        entry = entry + jnp.where(here, place * held * ROWS, 0)
    slot = jnp.arange(top_k, dtype=jnp.int32)
    before = (slot[:, None] < slot[None, :]) & match[..., :, None]
    rank = jnp.sum(before.astype(jnp.int32), axis=-2)
    rank = jnp.where(match, rank, -1)
    front = jnp.sum(jnp.where(rank[..., :, None] == slot, entry[..., :, None], 0), axis=-2)
    count = jnp.sum(match.astype(jnp.int32), axis=-1, keepdims=True)
    return jnp.concatenate([front, count], axis=-1).astype(jnp.int32)


def swap(value, axis, bit):
    return lax.ppermute(value, axis, [(i, i ^ bit) for i in range(lax.axis_size(axis))])


def shift(value, axis, steps):
    count = lax.axis_size(axis)
    return lax.ppermute(value, axis, [(i, (i + steps) % count) for i in range(count)])


def spread(value, axis, wraps):
    count = lax.axis_size(axis)
    reach = [count // 2, (count - 1) // 2] if wraps else [count - 1, count - 1]
    held = [value, value]
    found = []
    for hop in range(1, max(reach) + 1):
        found.append([])
        for side, sign in enumerate((1, -1)):
            if hop > reach[side]:
                continue
            pairs = []
            for source in range(count):
                target = source + sign
                if wraps:
                    pairs.append((source, target % count))
                elif 0 <= target < count and 0 <= target - sign * hop < count:
                    pairs.append((source, target))
            held[side] = lax.ppermute(held[side], axis, pairs)
            found[-1].append((held[side], -sign * hop))
    return found


def shards(wraps, queries, suffix_kv, prefix_kv, pooling, gate_logits, selected, lengths, w_out):
    rows = queries.shape[1]
    sib_count, ctx_count, head_count = (lax.axis_size(a) for a in ("sib", "ctx", "head"))
    blocks = rows // BLK
    sib, ctx, head = (lax.axis_index(a) for a in ("sib", "ctx", "head"))
    held_blocks = prefix_kv.shape[0] // BLK

    flat = queries.reshape(rows, HQ * DK)
    ids = selected.reshape(blocks, -1)
    packed, comp = pack(prefix_kv[:, 0, :].T, pooling)
    run_ids = [ids] + [shift(ids, "ctx", -d) for d in range(1, ctx_count)]
    bit = 1
    while bit < ctx_count:
        comp = jnp.concatenate([comp, swap(comp, "ctx", bit)], axis=0)
        bit *= 2
    flat, own_t, _ = lax.optimization_barrier((flat, suffix_kv[0, :, 0, :].T, comp))
    flats = [flat] + [shift(flat, "ctx", -d) for d in range(1, ctx_count)]
    far_t = lax.ppermute(own_t, "ctx", [(i, i + 1) for i in range(ctx_count - 1)])

    hops = [[(packed, 0)]] + spread(packed, "sib", wraps)
    for number, bit in enumerate(1 << k for k in range((sib_count - 1).bit_length())):
        got = swap(comp, "sib", bit)
        behind = [a for a, _ in hops[min(number + 1, len(hops) - 1)]]
        comp, got = lax.optimization_barrier((comp, got, behind))[:2]
        comp = jnp.concatenate([comp, got], axis=0)

    def owner_of(steps):
        other = sib + steps
        if wraps:
            other = other % sib_count
        good = (other >= 0) & (other < sib_count)
        return jnp.where(good, other * ctx_count + ctx, -2)

    levels = [hops[0] + hops[1]] + hops[2:]
    lists = [held_lists(jnp.stack(run_ids), [owner_of(t) for _, t in level], held_blocks) for level in levels]

    begin = (ctx * rows).astype(jnp.int32)
    gates = jax.nn.sigmoid(gate_logits.reshape(rows, 3, HQ))
    alive = begin + jnp.arange(rows, dtype=jnp.int32) < lengths[0]
    gates = jnp.where(alive[:, None, None], gates, 0.0)
    gates = gates.reshape(blocks, BLK, 3, HQ).transpose(0, 2, 3, 1).reshape(blocks, 3, HQ * BLK)

    wides = [wide_queries(f) for f in flats]
    near = near_parts(begin.reshape(1), wides[0], far_t, own_t, comp, gates)
    states = [None] * ctx_count
    for level, table in zip(levels[:-1], lists[:-1]):
        for run in range(ctx_count):
            states[run] = stage(UNIT, table[run], wides[run], [a for a, _ in level], states[run])
    table = lax.optimization_barrier((lists[-1], near, states))[0]
    kvs = [a for a, _ in levels[-1]]

    half = head_count // 2
    chunk = rows // head_count
    per = chunk // BLK
    high, low = head // half, head % half

    def half_order(which):
        starts = [(which * half + (low ^ k)) * per for k in range(half - 1, -1, -1)]
        return jnp.concatenate([s + jnp.arange(per, dtype=jnp.int32) for s in starts])

    orders = [half_order(1 - high), half_order(high)]
    parts = [
        [part_stage(UNIT, order, table[run], wides[run], kvs, states[run]) for run in range(1, ctx_count)]
        for order in orders
    ]
    others = [[shift(p, "ctx", d + 1) for d, p in enumerate(ps)] for ps in parts]
    orders[0] = lax.optimization_barrier((orders[0], parts[1]))[0]

    def half_sum(which):
        out = last_stage(
            UNIT, orders[which], table[0], wides[0], kvs, states[0], near, gates, others[which]
        )
        share = jnp.dot(out, w_out, preferred_element_type=F32)
        size = chunk // PIECES
        pieces = [share[k * size : (k + 1) * size].astype(BF) for k in range(PIECES)]
        other = jnp.concatenate([swap(piece, "head", 1) for piece in pieces], axis=0)
        return share[chunk:] + other.astype(F32)

    away = half_sum(0)
    away = away.astype(BF)
    back = swap(away, "head", half)
    orders[1] = lax.optimization_barrier((orders[1], away))[0]
    mine = half_sum(1)
    return (mine + back.astype(F32)).astype(BF).reshape(1, chunk, DM)


def solution(mesh):
    wraps = mesh.size >= 128
    return jax.shard_map(
        functools.partial(shards, wraps),
        mesh=mesh,
        in_specs=(
            P("sib", "ctx", "head", None),
            P("sib", "ctx", "head", None),
            P(("sib", "ctx"), "head", None),
            P(),
            P("sib", "ctx", "head", None),
            P("sib", "ctx", "head", None),
            P("sib"),
            P("head", None),
        ),
        out_specs=P("sib", ("ctx", "head"), None),
        check_vma=False,
    )
```

```python
import functools

import jax
import jax.numpy as jnp
from jax import lax
from jax.experimental import pallas as pl
from jax.experimental.pallas import tpu as pltpu
from jax.sharding import PartitionSpec as P

DK = 192
DV = 128
HQ = 8
DM = 2560
BLK = 64
W = 512
LANES = 128
TAIL = DK - LANES
EXT = 2 * LANES
ROWS = BLK + BLK // 2 + BLK
UNIT = 4
NOTES = 16
PIECES = 2
SCALE = DK ** (-0.5)
LOW = -1e30
VMEM = 32 * 1024 * 1024
BF = jnp.bfloat16
F32 = jnp.float32


def params(**more):
    return pltpu.CompilerParams(vmem_limit_bytes=VMEM, **more)


def cost(microseconds):
    return pl.CostEstimate(flops=int(microseconds * 1e9), bytes_accessed=0, transcendentals=0)


def lane_is_low(shape):
    return lax.broadcasted_iota(jnp.int32, shape, len(shape) - 1) < TAIL


def pack_kernel(kv_ref, pool_ref, packed_ref, comp_ref):
    tokens = kv_ref.shape[1]
    pool_key, pool_value = (
        jnp.broadcast_to(pool_ref[k : k + 1, :], (LANES, BLK)).T for k in range(2)
    )
    half = BLK // 2
    pool_tail = jnp.where(lane_is_low((half, LANES)), pool_key[:half], pool_key[half:])
    rows = []
    for tile in range(tokens // LANES):
        part = kv_ref[:, tile * LANES : (tile + 1) * LANES].astype(F32)
        keys = part[:LANES].T
        ends = part[LANES:DK]
        ends = jnp.concatenate([ends, pltpu.roll(ends, LANES - half, 1)], axis=0).T
        values = part[DK:].T
        for sub in range(LANES // BLK):
            base = (tile * (LANES // BLK) + sub) * ROWS
            at = sub * BLK
            key, end, value = keys[at : at + BLK], ends[at : at + half], values[at : at + BLK]
            packed_ref[base : base + BLK] = key.astype(BF)
            packed_ref[base + BLK : base + BLK + half] = end.astype(BF)
            packed_ref[base + BLK + half : base + ROWS] = value.astype(BF)
            comp_key = jnp.sum(key * pool_key, axis=0, keepdims=True)
            comp_end = jnp.sum(end * pool_tail, axis=0, keepdims=True)
            comp_end = comp_end + pltpu.roll(comp_end, TAIL, 1)
            comp_end = jnp.where(lane_is_low((1, LANES)), comp_end, 0.0)
            comp_value = jnp.sum(value * pool_value, axis=0, keepdims=True)
            rows.append(jnp.concatenate([comp_key, comp_end, comp_value], axis=1))
    comp_ref[...] = jnp.concatenate(rows, axis=0).astype(BF)


def pack(kv_t, pooling):
    blocks = kv_t.shape[1] // BLK
    return pl.pallas_call(
        pack_kernel,
        out_shape=(
            jax.ShapeDtypeStruct((blocks * ROWS, LANES), BF),
            jax.ShapeDtypeStruct((blocks, EXT + DV), BF),
        ),
        compiler_params=params(),
        cost_estimate=cost(5),
        name="pack",
    )(kv_t, pooling)


def wide_queries_kernel(q_ref, out_ref):
    low = lane_is_low((BLK, LANES))
    for pair in range(HQ // 2):
        at = pair * 2 * DK
        first, middle, last = (
            q_ref[:, at + k * LANES : at + (k + 1) * LANES].astype(F32) for k in range(3)
        )
        middle_swap = pltpu.roll(middle, TAIL, 1)
        last_swap = pltpu.roll(last, TAIL, 1)
        top = pair * 2 * BLK
        out_ref[0, top : top + BLK, :LANES] = first.astype(BF)
        out_ref[0, top : top + BLK, LANES:] = jnp.where(low, middle, middle_swap).astype(BF)
        top += BLK
        out_ref[0, top : top + BLK, :LANES] = jnp.where(low, middle_swap, last_swap).astype(BF)
        out_ref[0, top : top + BLK, LANES:] = jnp.where(low, last_swap, last).astype(BF)


def wide_queries(queries):
    rows = queries.shape[0]
    return pl.pallas_call(
        wide_queries_kernel,
        grid=(rows // BLK,),
        in_specs=[pl.BlockSpec((BLK, HQ * DK), lambda i: (i, 0))],
        out_specs=pl.BlockSpec((1, HQ * BLK, EXT), lambda i: (i, 0, 0)),
        out_shape=jax.ShapeDtypeStruct((rows // BLK, HQ * BLK, EXT), BF),
        compiler_params=params(),
        cost_estimate=cost(6),
        name="wide_queries",
    )(queries)


def scores_of(keys, queries):
    return lax.dot_general(keys, queries, (((1,), (1,)), ((), ())), preferred_element_type=F32)


def near_kernel(begin_ref, q_ref, far_ref, own_ref, comp_ref, gate_ref, out_ref, key_ref, value_ref):
    step = pl.program_id(0)
    rows = own_ref.shape[1]

    @pl.when(step == 0)
    def _():
        zeros = jnp.zeros((LANES, TAIL), BF)
        for source, top in ((far_ref, 0), (own_ref, rows)):
            for at in range(0, rows, LANES):
                part = source[:DK, at : at + LANES].astype(F32)
                key_ref[top + at : top + at + LANES, :LANES] = part[:LANES].T.astype(BF)
                end = jnp.concatenate([part[LANES:], jnp.zeros((TAIL, LANES), F32)], axis=0)
                key_ref[top + at : top + at + LANES, LANES:] = end.T.astype(BF)
            value_ref[:, top : top + rows] = source[DK:, :]

    queries = q_ref[0]
    gates = gate_ref[0]
    total_lanes = queries.shape[0]
    scores = scores_of(comp_ref[:, :EXT], queries)
    top = jnp.max(scores, axis=0, keepdims=True)
    weights = jnp.exp((scores - top) * SCALE)
    total = jnp.sum(weights, axis=0, keepdims=True)
    comp_out = lax.dot_general(
        comp_ref[:, EXT:], weights.astype(BF), (((0,), (0,)), ((), ())), preferred_element_type=F32
    )
    out = comp_out * (gates[0:1] / total)

    span = W + LANES
    start = pl.multiple_of((step // 2) * LANES + rows - W, LANES)
    scores = scores_of(key_ref[pl.ds(start, span), :], queries)
    key_pos = start - rows + lax.broadcasted_iota(jnp.int32, (span, total_lanes), 0)
    query_pos = step * BLK + (lax.broadcasted_iota(jnp.int32, (span, total_lanes), 1) & (BLK - 1))
    visible = (key_pos <= query_pos) & (key_pos > query_pos - W) & (key_pos + begin_ref[0] >= 0)
    scores = jnp.where(visible, scores, LOW)
    top = jnp.max(scores, axis=0, keepdims=True)
    weights = jnp.exp((scores - top) * SCALE)
    total = jnp.sum(weights, axis=0, keepdims=True)
    window_out = jnp.dot(
        value_ref[:, pl.ds(start, span)], weights.astype(BF), preferred_element_type=F32
    )
    out_ref[0] = out + window_out * (gates[2:3] / total)


def near_parts(begin, wide, far_t, own_t, comp, gates):
    steps, lanes, _ = wide.shape
    rows = own_t.shape[1]
    whole = lambda array: pl.BlockSpec(array.shape, lambda i, *_: (0,) * array.ndim)
    return pl.pallas_call(
        near_kernel,
        grid_spec=pltpu.PrefetchScalarGridSpec(
            num_scalar_prefetch=1,
            grid=(steps,),
            in_specs=[
                pl.BlockSpec((1, lanes, EXT), lambda i, *_: (i, 0, 0)),
                whole(far_t),
                whole(own_t),
                whole(comp),
                pl.BlockSpec((1, 3, lanes), lambda i, *_: (i, 0, 0)),
            ],
            out_specs=pl.BlockSpec((1, DV, lanes), lambda i, *_: (i, 0, 0)),
            scratch_shapes=[pltpu.VMEM((2 * rows, EXT), BF), pltpu.VMEM((DV, 2 * rows), BF)],
        ),
        out_shape=jax.ShapeDtypeStruct((steps, DV, lanes), F32),
        compiler_params=params(),
        cost_estimate=cost(14),
        name="near",
    )(begin, wide, far_t, own_t, comp, gates)


def add_selected(unit, list_ref, block, q_ref, kv_refs, top, total, acc_ref, key_ref, value_ref):
    count = list_ref[block, list_ref.shape[1] - 1]
    held = kv_refs[0].shape[0]
    half = BLK // 2
    low = lane_is_low((half, LANES))

    def step(index, state):
        top, total = state
        for k in range(unit):
            entry = list_ref[block, jnp.minimum(index * unit + k, count - 1)]
            for place, kv_ref in enumerate(kv_refs):
                inside = (entry >= place * held) & (entry < (place + 1) * held)

                @pl.when(inside)
                def _(kv_ref=kv_ref, place=place):
                    base = pl.multiple_of(entry - place * held, 32)
                    to = k * BLK
                    key_ref[to : to + BLK, :LANES] = kv_ref[pl.ds(base, BLK), :]
                    end = kv_ref[pl.ds(base + BLK, half), :]
                    zero = jnp.zeros_like(end)
                    key_ref[to : to + half, LANES:] = jnp.where(low, end, zero)
                    key_ref[to + half : to + BLK, LANES:] = jnp.where(low, zero, end)
                    value_ref[to : to + BLK, :] = kv_ref[pl.ds(base + BLK + half, BLK), :]

        keys = unit * BLK
        scores = scores_of(key_ref[:keys], q_ref[0])
        row = lax.broadcasted_iota(jnp.int32, scores.shape, 0)
        scores = jnp.where(row < (count - index * unit) * BLK, scores, LOW)
        new_top = jnp.maximum(top, jnp.max(scores, axis=0, keepdims=True))
        weights = jnp.exp((scores - new_top) * SCALE)
        keep = jnp.exp((top - new_top) * SCALE)
        total = total * keep + jnp.sum(weights, axis=0, keepdims=True)
        acc_ref[...] = acc_ref[...] * keep + lax.dot_general(
            value_ref[:keys],
            weights.astype(BF),
            (((0,), (0,)), ((), ())),
            preferred_element_type=F32,
        )
        return new_top, total

    return lax.fori_loop(0, (count + unit - 1) // unit, step, (top, total))


def scratch(unit):
    return [pltpu.VMEM((unit * BLK, EXT), BF), pltpu.VMEM((unit * BLK, DV), BF)]


def whole_spec(array):
    return pl.BlockSpec(array.shape, lambda i, *_: (0,) * array.ndim)


def stage_kernel(first, n_kv, unit, list_ref, q_ref, *refs):
    kv_refs, refs = refs[:n_kv], refs[n_kv:]
    lanes = q_ref.shape[1]
    if first:
        state_out, acc_out, key_ref, value_ref = refs
        top = jnp.full((1, lanes), LOW, F32)
        total = jnp.zeros((1, lanes), F32)
        acc_out[...] = jnp.zeros_like(acc_out)
    else:
        state_in, acc_in, state_out, acc_out, key_ref, value_ref = refs
        top, total = state_in[0, 0:1], state_in[0, 1:2]
        acc_out[...] = acc_in[...]
    top, total = add_selected(
        unit, list_ref, pl.program_id(0), q_ref, kv_refs, top, total, acc_out.at[0], key_ref, value_ref
    )
    state_out[0, 0:1] = top
    state_out[0, 1:2] = total


def stage(unit, lists, wide, kvs, state):
    steps, lanes, _ = wide.shape
    row = pl.BlockSpec((1, 2, lanes), lambda i, *_: (i, 0, 0))
    wide_row = pl.BlockSpec((1, DV, lanes), lambda i, *_: (i, 0, 0))
    in_specs = [pl.BlockSpec((1, lanes, EXT), lambda i, *_: (i, 0, 0))]
    in_specs += [whole_spec(kv) for kv in kvs]
    first = state is None
    aliases = {}
    if not first:
        in_specs += [row, wide_row]
        aliases = {2 + len(kvs): 0, 3 + len(kvs): 1}
    return pl.pallas_call(
        functools.partial(stage_kernel, first, len(kvs), unit),
        grid_spec=pltpu.PrefetchScalarGridSpec(
            num_scalar_prefetch=1,
            grid=(steps,),
            in_specs=in_specs,
            out_specs=[row, wide_row],
            scratch_shapes=scratch(unit),
        ),
        out_shape=(
            jax.ShapeDtypeStruct((steps, 2, lanes), F32),
            jax.ShapeDtypeStruct((steps, DV, lanes), F32),
        ),
        input_output_aliases=aliases,
        compiler_params=params(),
        cost_estimate=cost(9),
        name="stage",
    )(lists, wide, *kvs, *(() if first else state))


def log_total(top, total):
    return jnp.where(total > 0, top * SCALE + jnp.log(jnp.maximum(total, 1e-30)), LOW)


def part_kernel(n_kv, unit, order_ref, list_ref, q_ref, *refs):
    kv_refs, refs = refs[:n_kv], refs[n_kv:]
    state_in, acc_in, out_ref, acc_ref, key_ref, value_ref = refs
    acc_ref[...] = acc_in[0]
    top, total = add_selected(
        unit,
        list_ref,
        order_ref[pl.program_id(0)],
        q_ref,
        kv_refs,
        state_in[0, 0:1],
        state_in[0, 1:2],
        acc_ref,
        key_ref,
        value_ref,
    )
    out_ref[0, :DV] = (acc_ref[...] / jnp.maximum(total, 1e-30)).astype(BF)
    rest = log_total(top, total)
    terms = []
    for _ in range(3):
        terms.append(rest.astype(BF).astype(F32))
        rest = rest - terms[-1]
    terms.append(jnp.zeros((NOTES - len(terms), rest.shape[1]), F32))
    out_ref[0, DV:] = jnp.concatenate(terms, axis=0).astype(BF)


def part_stage(unit, order, lists, wide, kvs, state):
    _, lanes, _ = wide.shape
    (steps,) = order.shape
    at = lambda i, order, *_: (order[i], 0, 0)
    return pl.pallas_call(
        functools.partial(part_kernel, len(kvs), unit),
        grid_spec=pltpu.PrefetchScalarGridSpec(
            num_scalar_prefetch=2,
            grid=(steps,),
            in_specs=[pl.BlockSpec((1, lanes, EXT), at)]
            + [whole_spec(kv) for kv in kvs]
            + [pl.BlockSpec((1, 2, lanes), at), pl.BlockSpec((1, DV, lanes), at)],
            out_specs=pl.BlockSpec((1, DV + NOTES, lanes), lambda i, *_: (i, 0, 0)),
            scratch_shapes=[pltpu.VMEM((DV, lanes), F32)] + scratch(unit),
        ),
        out_shape=jax.ShapeDtypeStruct((steps, DV + NOTES, lanes), BF),
        compiler_params=params(),
        cost_estimate=cost(4),
        name="part_stage",
    )(order, lists, wide, *kvs, *state)


def last_kernel(order_ref, state_ref, acc_ref, near_ref, gate_ref, *refs):
    part_refs, out_ref = refs[:-1], refs[-1]
    total = state_ref[0, 1:2]
    logs = [log_total(state_ref[0, 0:1], total)]
    for part_ref in part_refs:
        notes = part_ref[0, DV:].astype(F32)
        logs.append(notes[0:1] + notes[1:2] + notes[2:3])
    peak = functools.reduce(jnp.maximum, logs)
    shares = [jnp.exp(log - peak) for log in logs]
    gate = gate_ref[0, 1:2] / functools.reduce(jnp.add, shares)
    out = near_ref[0] + acc_ref[0] * (gate * shares[0] / jnp.maximum(total, 1e-30))
    for share, part_ref in zip(shares[1:], part_refs):
        out = out + part_ref[0, :DV].astype(F32) * (gate * share)
    for head in range(0, HQ, 2):
        pair = out[:, head * BLK : (head + 2) * BLK].T.astype(BF)
        out_ref[:, head * DV : (head + 1) * DV] = pair[:BLK]
        out_ref[:, (head + 1) * DV : (head + 2) * DV] = pair[BLK:]


def last_stage(order, state, near, gates, others):
    lanes = near.shape[2]
    (steps,) = order.shape
    at = lambda i, order: (order[i], 0, 0)
    return pl.pallas_call(
        last_kernel,
        grid_spec=pltpu.PrefetchScalarGridSpec(
            num_scalar_prefetch=1,
            grid=(steps,),
            in_specs=[
                pl.BlockSpec((1, 2, lanes), at),
                pl.BlockSpec((1, DV, lanes), at),
                pl.BlockSpec((1, DV, lanes), at),
                pl.BlockSpec((1, 3, lanes), at),
            ]
            + [pl.BlockSpec((1, DV + NOTES, lanes), lambda i, order: (i, 0, 0)) for _ in others],
            out_specs=pl.BlockSpec((BLK, HQ * DV), lambda i, order: (i, 0)),
        ),
        out_shape=jax.ShapeDtypeStruct((steps * BLK, HQ * DV), BF),
        compiler_params=params(),
        cost_estimate=cost(5),
        name="last_stage",
    )(order, *state, near, gates, *others)


def held_lists(ids, owners, held):
    top_k = ids.shape[-1]
    owner = ids // held
    entry = (ids % held) * ROWS
    match = jnp.zeros(ids.shape, jnp.bool_)
    for place, one in enumerate(owners):
        here = owner == one
        match = match | here
        entry = entry + jnp.where(here, place * held * ROWS, 0)
    slot = jnp.arange(top_k, dtype=jnp.int32)
    before = (slot[:, None] < slot[None, :]) & match[..., :, None]
    rank = jnp.sum(before.astype(jnp.int32), axis=-2)
    rank = jnp.where(match, rank, -1)
    front = jnp.sum(jnp.where(rank[..., :, None] == slot, entry[..., :, None], 0), axis=-2)
    count = jnp.sum(match.astype(jnp.int32), axis=-1, keepdims=True)
    return jnp.concatenate([front, count], axis=-1).astype(jnp.int32)


def swap(value, axis, bit):
    return lax.ppermute(value, axis, [(i, i ^ bit) for i in range(lax.axis_size(axis))])


def shift(value, axis, steps):
    count = lax.axis_size(axis)
    return lax.ppermute(value, axis, [(i, (i + steps) % count) for i in range(count)])


def spread(value, axis, wraps):
    count = lax.axis_size(axis)
    reach = [count // 2, (count - 1) // 2] if wraps else [count - 1, count - 1]
    held = [value, value]
    found = []
    for hop in range(1, max(reach) + 1):
        found.append([])
        for side, sign in enumerate((1, -1)):
            if hop > reach[side]:
                continue
            pairs = []
            for source in range(count):
                target = source + sign
                if wraps:
                    pairs.append((source, target % count))
                elif 0 <= target < count and 0 <= target - sign * hop < count:
                    pairs.append((source, target))
            held[side] = lax.ppermute(held[side], axis, pairs)
            found[-1].append((held[side], -sign * hop))
    return found


def shards(wraps, queries, suffix_kv, prefix_kv, pooling, gate_logits, selected, lengths, w_out):
    rows = queries.shape[1]
    sib_count, ctx_count, head_count = (lax.axis_size(a) for a in ("sib", "ctx", "head"))
    blocks = rows // BLK
    sib, ctx, head = (lax.axis_index(a) for a in ("sib", "ctx", "head"))
    held_blocks = prefix_kv.shape[0] // BLK

    flat = queries.reshape(rows, HQ * DK)
    ids = selected.reshape(blocks, -1)
    packed, comp = pack(prefix_kv[:, 0, :].T, pooling)
    run_ids = [ids] + [shift(ids, "ctx", -d) for d in range(1, ctx_count)]
    bit = 1
    while bit < ctx_count:
        comp = jnp.concatenate([comp, swap(comp, "ctx", bit)], axis=0)
        bit *= 2
    flat, own_t, _ = lax.optimization_barrier((flat, suffix_kv[0, :, 0, :].T, comp))
    flats = [flat] + [shift(flat, "ctx", -d) for d in range(1, ctx_count)]
    far_t = lax.ppermute(own_t, "ctx", [(i, i + 1) for i in range(ctx_count - 1)])

    hops = [[(packed, 0)]] + spread(packed, "sib", wraps)
    for number, bit in enumerate(1 << k for k in range((sib_count - 1).bit_length())):
        got = swap(comp, "sib", bit)
        behind = [a for a, _ in hops[min(number + 1, len(hops) - 1)]]
        comp, got = lax.optimization_barrier((comp, got, behind))[:2]
        comp = jnp.concatenate([comp, got], axis=0)

    def owner_of(steps):
        other = sib + steps
        if wraps:
            other = other % sib_count
        good = (other >= 0) & (other < sib_count)
        return jnp.where(good, other * ctx_count + ctx, -2)

    levels = [hops[0] + hops[1]] + hops[2:]
    lists = [held_lists(jnp.stack(run_ids), [owner_of(t) for _, t in level], held_blocks) for level in levels]

    begin = (ctx * rows).astype(jnp.int32)
    gates = jax.nn.sigmoid(gate_logits.reshape(rows, 3, HQ))
    alive = begin + jnp.arange(rows, dtype=jnp.int32) < lengths[0]
    gates = jnp.where(alive[:, None, None], gates, 0.0)
    gates = gates.reshape(blocks, BLK, 3, HQ).transpose(0, 2, 3, 1).reshape(blocks, 3, HQ * BLK)

    wides = [wide_queries(f) for f in flats]
    near = near_parts(begin.reshape(1), wides[0], far_t, own_t, comp, gates)
    states = [None] * ctx_count
    for level, table in zip(levels[:-1], lists[:-1]):
        for run in range(ctx_count):
            states[run] = stage(UNIT, table[run], wides[run], [a for a, _ in level], states[run])
    table = lax.optimization_barrier((lists[-1], near, states))[0]
    kvs = [a for a, _ in levels[-1]]

    half = head_count // 2
    chunk = rows // head_count
    per = chunk // BLK
    high, low = head // half, head % half

    def half_order(which):
        starts = [(which * half + (low ^ k)) * per for k in range(half - 1, -1, -1)]
        return jnp.concatenate([s + jnp.arange(per, dtype=jnp.int32) for s in starts])

    orders = [half_order(1 - high), half_order(high)]
    parts = [
        [part_stage(UNIT, order, table[run], wides[run], kvs, states[run]) for run in range(1, ctx_count)]
        for order in orders
    ]
    others = [[shift(p, "ctx", d + 1) for d, p in enumerate(ps)] for ps in parts]
    mine_table = lax.optimization_barrier((table[0], parts[1]))[0]
    state = stage(UNIT, mine_table, wides[0], kvs, states[0])

    def half_sum(which):
        out = last_stage(orders[which], state, near, gates, others[which])
        share = jnp.dot(out, w_out, preferred_element_type=F32)
        size = chunk // PIECES
        pieces = [share[k * size : (k + 1) * size].astype(BF) for k in range(PIECES)]
        other = jnp.concatenate([swap(piece, "head", 1) for piece in pieces], axis=0)
        return share[chunk:] + other.astype(F32)

    away = half_sum(0)
    away = away.astype(BF)
    back = swap(away, "head", half)
    orders[1] = lax.optimization_barrier((orders[1], away))[0]
    mine = half_sum(1)
    return (mine + back.astype(F32)).astype(BF).reshape(1, chunk, DM)


def solution(mesh):
    wraps = mesh.size >= 128
    return jax.shard_map(
        functools.partial(shards, wraps),
        mesh=mesh,
        in_specs=(
            P("sib", "ctx", "head", None),
            P("sib", "ctx", "head", None),
            P(("sib", "ctx"), "head", None),
            P(),
            P("sib", "ctx", "head", None),
            P("sib", "ctx", "head", None),
            P("sib"),
            P("head", None),
        ),
        out_specs=P("sib", ("ctx", "head"), None),
        check_vma=False,
    )
```

```python
import functools

import jax
import jax.numpy as jnp
from jax import lax
from jax.experimental import pallas as pl
from jax.experimental.pallas import tpu as pltpu
from jax.sharding import PartitionSpec as P

DK = 192
DV = 128
HQ = 8
DM = 2560
BLK = 64
W = 512
LANES = 128
TAIL = DK - LANES
EXT = 2 * LANES
ROWS = BLK + BLK // 2 + BLK
UNIT = 4
NOTES = 16
PIECES = 2
SCALE = DK ** (-0.5)
LOW = -1e30
VMEM = 32 * 1024 * 1024
BF = jnp.bfloat16
F32 = jnp.float32


def params(**more):
    return pltpu.CompilerParams(vmem_limit_bytes=VMEM, **more)


def cost(microseconds):
    return pl.CostEstimate(flops=int(microseconds * 1e9), bytes_accessed=0, transcendentals=0)


def lane_is_low(shape):
    return lax.broadcasted_iota(jnp.int32, shape, len(shape) - 1) < TAIL


def pack_kernel(kv_ref, pool_ref, packed_ref, comp_ref):
    tokens = kv_ref.shape[1]
    pool_key, pool_value = (
        jnp.broadcast_to(pool_ref[k : k + 1, :], (LANES, BLK)).T for k in range(2)
    )
    half = BLK // 2
    pool_tail = jnp.where(lane_is_low((half, LANES)), pool_key[:half], pool_key[half:])
    rows = []
    for tile in range(tokens // LANES):
        part = kv_ref[:, tile * LANES : (tile + 1) * LANES].astype(F32)
        keys = part[:LANES].T
        ends = part[LANES:DK]
        ends = jnp.concatenate([ends, pltpu.roll(ends, LANES - half, 1)], axis=0).T
        values = part[DK:].T
        for sub in range(LANES // BLK):
            base = (tile * (LANES // BLK) + sub) * ROWS
            at = sub * BLK
            key, end, value = keys[at : at + BLK], ends[at : at + half], values[at : at + BLK]
            packed_ref[base : base + BLK] = key.astype(BF)
            packed_ref[base + BLK : base + BLK + half] = end.astype(BF)
            packed_ref[base + BLK + half : base + ROWS] = value.astype(BF)
            comp_key = jnp.sum(key * pool_key, axis=0, keepdims=True)
            comp_end = jnp.sum(end * pool_tail, axis=0, keepdims=True)
            comp_end = comp_end + pltpu.roll(comp_end, TAIL, 1)
            comp_end = jnp.where(lane_is_low((1, LANES)), comp_end, 0.0)
            comp_value = jnp.sum(value * pool_value, axis=0, keepdims=True)
            rows.append(jnp.concatenate([comp_key, comp_end, comp_value], axis=1))
    comp_ref[...] = jnp.concatenate(rows, axis=0).astype(BF)


def pack(kv_t, pooling):
    depth, tokens = kv_t.shape
    blocks = tokens // BLK
    part = NOTES
    return pl.pallas_call(
        pack_kernel,
        grid=(blocks // part,),
        in_specs=[
            pl.BlockSpec((depth, part * BLK), lambda i: (0, i)),
            pl.BlockSpec(pooling.shape, lambda i: (0, 0)),
        ],
        out_specs=(
            pl.BlockSpec((part * ROWS, LANES), lambda i: (i, 0)),
            pl.BlockSpec((part, EXT + DV), lambda i: (i, 0)),
        ),
        out_shape=(
            jax.ShapeDtypeStruct((blocks * ROWS, LANES), BF),
            jax.ShapeDtypeStruct((blocks, EXT + DV), BF),
        ),
        compiler_params=params(),
        cost_estimate=cost(5),
        name="pack",
    )(kv_t, pooling)


def wide_queries_kernel(q_ref, out_ref):
    low = lane_is_low((BLK, LANES))
    for pair in range(HQ // 2):
        at = pair * 2 * DK
        first, middle, last = (
            q_ref[:, at + k * LANES : at + (k + 1) * LANES].astype(F32) for k in range(3)
        )
        middle_swap = pltpu.roll(middle, TAIL, 1)
        last_swap = pltpu.roll(last, TAIL, 1)
        top = pair * 2 * BLK
        out_ref[0, top : top + BLK, :LANES] = first.astype(BF)
        out_ref[0, top : top + BLK, LANES:] = jnp.where(low, middle, middle_swap).astype(BF)
        top += BLK
        out_ref[0, top : top + BLK, :LANES] = jnp.where(low, middle_swap, last_swap).astype(BF)
        out_ref[0, top : top + BLK, LANES:] = jnp.where(low, last_swap, last).astype(BF)


def wide_queries(queries):
    rows = queries.shape[0]
    return pl.pallas_call(
        wide_queries_kernel,
        grid=(rows // BLK,),
        in_specs=[pl.BlockSpec((BLK, HQ * DK), lambda i: (i, 0))],
        out_specs=pl.BlockSpec((1, HQ * BLK, EXT), lambda i: (i, 0, 0)),
        out_shape=jax.ShapeDtypeStruct((rows // BLK, HQ * BLK, EXT), BF),
        compiler_params=params(),
        cost_estimate=cost(6),
        name="wide_queries",
    )(queries)


def scores_of(keys, queries):
    return lax.dot_general(keys, queries, (((1,), (1,)), ((), ())), preferred_element_type=F32)


def near_kernel(begin_ref, q_ref, far_ref, own_ref, comp_ref, gate_ref, out_ref, key_ref, value_ref):
    step = pl.program_id(0)
    rows = own_ref.shape[1]

    @pl.when(step == 0)
    def _():
        zeros = jnp.zeros((LANES, TAIL), BF)
        for source, top in ((far_ref, 0), (own_ref, rows)):
            for at in range(0, rows, LANES):
                part = source[:DK, at : at + LANES].astype(F32)
                key_ref[top + at : top + at + LANES, :LANES] = part[:LANES].T.astype(BF)
                end = jnp.concatenate([part[LANES:], jnp.zeros((TAIL, LANES), F32)], axis=0)
                key_ref[top + at : top + at + LANES, LANES:] = end.T.astype(BF)
            value_ref[:, top : top + rows] = source[DK:, :]

    queries = q_ref[0]
    gates = gate_ref[0]
    total_lanes = queries.shape[0]
    scores = scores_of(comp_ref[:, :EXT], queries)
    top = jnp.max(scores, axis=0, keepdims=True)
    weights = jnp.exp((scores - top) * SCALE)
    total = jnp.sum(weights, axis=0, keepdims=True)
    comp_out = lax.dot_general(
        comp_ref[:, EXT:], weights.astype(BF), (((0,), (0,)), ((), ())), preferred_element_type=F32
    )
    out = comp_out * (gates[0:1] / total)

    span = W + LANES
    start = pl.multiple_of((step // 2) * LANES + rows - W, LANES)
    scores = scores_of(key_ref[pl.ds(start, span), :], queries)
    key_pos = start - rows + lax.broadcasted_iota(jnp.int32, (span, total_lanes), 0)
    query_pos = step * BLK + (lax.broadcasted_iota(jnp.int32, (span, total_lanes), 1) & (BLK - 1))
    visible = (key_pos <= query_pos) & (key_pos > query_pos - W) & (key_pos + begin_ref[0] >= 0)
    scores = jnp.where(visible, scores, LOW)
    top = jnp.max(scores, axis=0, keepdims=True)
    weights = jnp.exp((scores - top) * SCALE)
    total = jnp.sum(weights, axis=0, keepdims=True)
    window_out = jnp.dot(
        value_ref[:, pl.ds(start, span)], weights.astype(BF), preferred_element_type=F32
    )
    out_ref[0] = out + window_out * (gates[2:3] / total)


def near_parts(begin, wide, far_t, own_t, comp, gates):
    steps, lanes, _ = wide.shape
    rows = own_t.shape[1]
    whole = lambda array: pl.BlockSpec(array.shape, lambda i, *_: (0,) * array.ndim)
    return pl.pallas_call(
        near_kernel,
        grid_spec=pltpu.PrefetchScalarGridSpec(
            num_scalar_prefetch=1,
            grid=(steps,),
            in_specs=[
                pl.BlockSpec((1, lanes, EXT), lambda i, *_: (i, 0, 0)),
                whole(far_t),
                whole(own_t),
                whole(comp),
                pl.BlockSpec((1, 3, lanes), lambda i, *_: (i, 0, 0)),
            ],
            out_specs=pl.BlockSpec((1, DV, lanes), lambda i, *_: (i, 0, 0)),
            scratch_shapes=[pltpu.VMEM((2 * rows, EXT), BF), pltpu.VMEM((DV, 2 * rows), BF)],
        ),
        out_shape=jax.ShapeDtypeStruct((steps, DV, lanes), F32),
        compiler_params=params(),
        cost_estimate=cost(14),
        name="near",
    )(begin, wide, far_t, own_t, comp, gates)


def add_selected(unit, list_ref, block, q_ref, kv_refs, top, total, acc_ref, key_ref, value_ref):
    count = list_ref[block, list_ref.shape[1] - 1]
    held = kv_refs[0].shape[0]
    half = BLK // 2
    low = lane_is_low((half, LANES))

    def step(index, state):
        top, total = state
        for k in range(unit):
            entry = list_ref[block, jnp.minimum(index * unit + k, count - 1)]
            for place, kv_ref in enumerate(kv_refs):
                inside = (entry >= place * held) & (entry < (place + 1) * held)

                @pl.when(inside)
                def _(kv_ref=kv_ref, place=place):
                    base = pl.multiple_of(entry - place * held, 32)
                    to = k * BLK
                    key_ref[to : to + BLK, :LANES] = kv_ref[pl.ds(base, BLK), :]
                    end = kv_ref[pl.ds(base + BLK, half), :]
                    zero = jnp.zeros_like(end)
                    key_ref[to : to + half, LANES:] = jnp.where(low, end, zero)
                    key_ref[to + half : to + BLK, LANES:] = jnp.where(low, zero, end)
                    value_ref[to : to + BLK, :] = kv_ref[pl.ds(base + BLK + half, BLK), :]

        keys = unit * BLK
        scores = scores_of(key_ref[:keys], q_ref[0])
        row = lax.broadcasted_iota(jnp.int32, scores.shape, 0)
        scores = jnp.where(row < (count - index * unit) * BLK, scores, LOW)
        new_top = jnp.maximum(top, jnp.max(scores, axis=0, keepdims=True))
        weights = jnp.exp((scores - new_top) * SCALE)
        keep = jnp.exp((top - new_top) * SCALE)
        total = total * keep + jnp.sum(weights, axis=0, keepdims=True)
        acc_ref[...] = acc_ref[...] * keep + lax.dot_general(
            value_ref[:keys],
            weights.astype(BF),
            (((0,), (0,)), ((), ())),
            preferred_element_type=F32,
        )
        return new_top, total

    return lax.fori_loop(0, (count + unit - 1) // unit, step, (top, total))


def scratch(unit):
    return [pltpu.VMEM((unit * BLK, EXT), BF), pltpu.VMEM((unit * BLK, DV), BF)]


def whole_spec(array):
    return pl.BlockSpec(array.shape, lambda i, *_: (0,) * array.ndim)


def stage_kernel(first, n_kv, unit, list_ref, q_ref, *refs):
    kv_refs, refs = refs[:n_kv], refs[n_kv:]
    lanes = q_ref.shape[1]
    if first:
        state_out, acc_out, key_ref, value_ref = refs
        top = jnp.full((1, lanes), LOW, F32)
        total = jnp.zeros((1, lanes), F32)
        acc_out[...] = jnp.zeros_like(acc_out)
    else:
        state_in, acc_in, state_out, acc_out, key_ref, value_ref = refs
        top, total = state_in[0, 0:1], state_in[0, 1:2]
        acc_out[...] = acc_in[...]
    top, total = add_selected(
        unit, list_ref, pl.program_id(0), q_ref, kv_refs, top, total, acc_out.at[0], key_ref, value_ref
    )
    state_out[0, 0:1] = top
    state_out[0, 1:2] = total


def stage(unit, lists, wide, kvs, state):
    steps, lanes, _ = wide.shape
    row = pl.BlockSpec((1, 2, lanes), lambda i, *_: (i, 0, 0))
    wide_row = pl.BlockSpec((1, DV, lanes), lambda i, *_: (i, 0, 0))
    in_specs = [pl.BlockSpec((1, lanes, EXT), lambda i, *_: (i, 0, 0))]
    in_specs += [whole_spec(kv) for kv in kvs]
    first = state is None
    aliases = {}
    if not first:
        in_specs += [row, wide_row]
        aliases = {2 + len(kvs): 0, 3 + len(kvs): 1}
    return pl.pallas_call(
        functools.partial(stage_kernel, first, len(kvs), unit),
        grid_spec=pltpu.PrefetchScalarGridSpec(
            num_scalar_prefetch=1,
            grid=(steps,),
            in_specs=in_specs,
            out_specs=[row, wide_row],
            scratch_shapes=scratch(unit),
        ),
        out_shape=(
            jax.ShapeDtypeStruct((steps, 2, lanes), F32),
            jax.ShapeDtypeStruct((steps, DV, lanes), F32),
        ),
        input_output_aliases=aliases,
        compiler_params=params(),
        cost_estimate=cost(9),
        name="stage",
    )(lists, wide, *kvs, *(() if first else state))


def log_total(top, total):
    return jnp.where(total > 0, top * SCALE + jnp.log(jnp.maximum(total, 1e-30)), LOW)


def part_kernel(n_kv, unit, order_ref, list_ref, q_ref, *refs):
    kv_refs, refs = refs[:n_kv], refs[n_kv:]
    state_in, acc_in, out_ref, acc_ref, notes_ref, key_ref, value_ref = refs
    acc_ref[...] = acc_in[0]
    top, total = add_selected(
        unit,
        list_ref,
        order_ref[pl.program_id(0)],
        q_ref,
        kv_refs,
        state_in[0, 0:1],
        state_in[0, 1:2],
        acc_ref,
        key_ref,
        value_ref,
    )
    step, steps = pl.program_id(0), pl.num_programs(0)
    at = pl.multiple_of(step * DV, DV)
    out_ref[pl.ds(at, DV), :] = (acc_ref[...] / jnp.maximum(total, 1e-30)).astype(BF)
    rest = log_total(top, total)
    row = lax.broadcasted_iota(jnp.int32, notes_ref.shape, 0)
    notes = jnp.where(step == 0, 0.0, notes_ref[...])
    for term in range(3):
        value = rest.astype(BF).astype(F32)
        notes = jnp.where(row == term * steps + step, value, notes)
        rest = rest - value
    notes_ref[...] = notes
    out_ref[out_ref.shape[0] - notes.shape[0] :, :] = notes.astype(BF)


def part_stage(unit, order, lists, wide, kvs, state):
    _, lanes, _ = wide.shape
    (steps,) = order.shape
    notes = -(-3 * steps // NOTES) * NOTES
    at = lambda i, order, *_: (order[i], 0, 0)
    return pl.pallas_call(
        functools.partial(part_kernel, len(kvs), unit),
        grid_spec=pltpu.PrefetchScalarGridSpec(
            num_scalar_prefetch=2,
            grid=(steps,),
            in_specs=[pl.BlockSpec((1, lanes, EXT), at)]
            + [whole_spec(kv) for kv in kvs]
            + [pl.BlockSpec((1, 2, lanes), at), pl.BlockSpec((1, DV, lanes), at)],
            out_specs=pl.BlockSpec((steps * DV + notes, lanes), lambda i, *_: (0, 0)),
            scratch_shapes=[pltpu.VMEM((DV, lanes), F32), pltpu.VMEM((notes, lanes), F32)]
            + scratch(unit),
        ),
        out_shape=jax.ShapeDtypeStruct((steps * DV + notes, lanes), BF),
        compiler_params=params(),
        cost_estimate=cost(4),
        name="part_stage",
    )(order, lists, wide, *kvs, *state)


def last_kernel(order_ref, state_ref, acc_ref, near_ref, gate_ref, *refs):
    part_refs, out_ref = refs[:-1], refs[-1]
    total = state_ref[0, 1:2]
    logs = [log_total(state_ref[0, 0:1], total)]
    step, steps = pl.program_id(0), pl.num_programs(0)
    at = pl.multiple_of(step * DV, DV)
    for part_ref in part_refs:
        notes = part_ref[part_ref.shape[0] // DV * DV :, :].astype(F32)
        row = lax.broadcasted_iota(jnp.int32, notes.shape, 0)
        here = functools.reduce(jnp.logical_or, [row == term * steps + step for term in range(3)])
        logs.append(jnp.sum(jnp.where(here, notes, 0.0), axis=0, keepdims=True))
    peak = functools.reduce(jnp.maximum, logs)
    shares = [jnp.exp(log - peak) for log in logs]
    gate = gate_ref[0, 1:2] / functools.reduce(jnp.add, shares)
    out = near_ref[0] + acc_ref[0] * (gate * shares[0] / jnp.maximum(total, 1e-30))
    for share, part_ref in zip(shares[1:], part_refs):
        out = out + part_ref[pl.ds(at, DV), :].astype(F32) * (gate * share)
    for head in range(0, HQ, 2):
        pair = out[:, head * BLK : (head + 2) * BLK].T.astype(BF)
        out_ref[:, head * DV : (head + 1) * DV] = pair[:BLK]
        out_ref[:, (head + 1) * DV : (head + 2) * DV] = pair[BLK:]


def last_stage(order, state, near, gates, others):
    lanes = near.shape[2]
    (steps,) = order.shape
    at = lambda i, order: (order[i], 0, 0)
    return pl.pallas_call(
        last_kernel,
        grid_spec=pltpu.PrefetchScalarGridSpec(
            num_scalar_prefetch=1,
            grid=(steps,),
            in_specs=[
                pl.BlockSpec((1, 2, lanes), at),
                pl.BlockSpec((1, DV, lanes), at),
                pl.BlockSpec((1, DV, lanes), at),
                pl.BlockSpec((1, 3, lanes), at),
            ]
            + [pl.BlockSpec(other.shape, lambda i, order: (0, 0)) for other in others],
            out_specs=pl.BlockSpec((BLK, HQ * DV), lambda i, order: (i, 0)),
        ),
        out_shape=jax.ShapeDtypeStruct((steps * BLK, HQ * DV), BF),
        compiler_params=params(),
        cost_estimate=cost(5),
        name="last_stage",
    )(order, *state, near, gates, *others)


def held_lists(ids, owners, held):
    top_k = ids.shape[-1]
    owner = ids // held
    entry = (ids % held) * ROWS
    match = jnp.zeros(ids.shape, jnp.bool_)
    for place, one in enumerate(owners):
        here = owner == one
        match = match | here
        entry = entry + jnp.where(here, place * held * ROWS, 0)
    slot = jnp.arange(top_k, dtype=jnp.int32)
    before = (slot[:, None] < slot[None, :]) & match[..., :, None]
    rank = jnp.sum(before.astype(jnp.int32), axis=-2)
    rank = jnp.where(match, rank, -1)
    front = jnp.sum(jnp.where(rank[..., :, None] == slot, entry[..., :, None], 0), axis=-2)
    count = jnp.sum(match.astype(jnp.int32), axis=-1, keepdims=True)
    return jnp.concatenate([front, count], axis=-1).astype(jnp.int32)


def swap(value, axis, bit):
    return lax.ppermute(value, axis, [(i, i ^ bit) for i in range(lax.axis_size(axis))])


def shift(value, axis, steps):
    count = lax.axis_size(axis)
    return lax.ppermute(value, axis, [(i, (i + steps) % count) for i in range(count)])


def spread(value, axis, wraps):
    count = lax.axis_size(axis)
    reach = [count // 2, (count - 1) // 2] if wraps else [count - 1, count - 1]
    held = [value, value]
    found = []
    for hop in range(1, max(reach) + 1):
        found.append([])
        for side, sign in enumerate((1, -1)):
            if hop > reach[side]:
                continue
            pairs = []
            for source in range(count):
                target = source + sign
                if wraps:
                    pairs.append((source, target % count))
                elif 0 <= target < count and 0 <= target - sign * hop < count:
                    pairs.append((source, target))
            held[side] = lax.ppermute(held[side], axis, pairs)
            found[-1].append((held[side], -sign * hop))
    return found


def shards(wraps, queries, suffix_kv, prefix_kv, pooling, gate_logits, selected, lengths, w_out):
    rows = queries.shape[1]
    sib_count, ctx_count, head_count = (lax.axis_size(a) for a in ("sib", "ctx", "head"))
    blocks = rows // BLK
    sib, ctx, head = (lax.axis_index(a) for a in ("sib", "ctx", "head"))
    held_blocks = prefix_kv.shape[0] // BLK

    flat = queries.reshape(rows, HQ * DK)
    ids = selected.reshape(blocks, -1)
    packed, comp = pack(prefix_kv[:, 0, :].T, pooling)
    run_ids = [ids] + [shift(ids, "ctx", -d) for d in range(1, ctx_count)]
    bit = 1
    while bit < ctx_count:
        comp = jnp.concatenate([comp, swap(comp, "ctx", bit)], axis=0)
        bit *= 2
    flat, own_t, _ = lax.optimization_barrier((flat, suffix_kv[0, :, 0, :].T, comp))
    flats = [flat] + [shift(flat, "ctx", -d) for d in range(1, ctx_count)]
    far_t = lax.ppermute(own_t, "ctx", [(i, i + 1) for i in range(ctx_count - 1)])

    hops = [[(packed, 0)]] + spread(packed, "sib", wraps)
    for number, bit in enumerate(1 << k for k in range((sib_count - 1).bit_length())):
        got = swap(comp, "sib", bit)
        behind = [a for a, _ in hops[min(number + 1, len(hops) - 1)]]
        comp, got = lax.optimization_barrier((comp, got, behind))[:2]
        comp = jnp.concatenate([comp, got], axis=0)

    def owner_of(steps):
        other = sib + steps
        if wraps:
            other = other % sib_count
        good = (other >= 0) & (other < sib_count)
        return jnp.where(good, other * ctx_count + ctx, -2)

    levels = [hops[0] + hops[1]] + hops[2:]
    lists = [held_lists(jnp.stack(run_ids), [owner_of(t) for _, t in level], held_blocks) for level in levels]

    begin = (ctx * rows).astype(jnp.int32)
    gates = jax.nn.sigmoid(gate_logits.reshape(rows, 3, HQ))
    alive = begin + jnp.arange(rows, dtype=jnp.int32) < lengths[0]
    gates = jnp.where(alive[:, None, None], gates, 0.0)
    gates = gates.reshape(blocks, BLK, 3, HQ).transpose(0, 2, 3, 1).reshape(blocks, 3, HQ * BLK)

    wides = [wide_queries(f) for f in flats]
    near = near_parts(begin.reshape(1), wides[0], far_t, own_t, comp, gates)
    states = [None] * ctx_count
    for level, table in zip(levels[:-1], lists[:-1]):
        for run in range(ctx_count):
            states[run] = stage(UNIT, table[run], wides[run], [a for a, _ in level], states[run])
    table = lax.optimization_barrier((lists[-1], near, states))[0]
    kvs = [a for a, _ in levels[-1]]

    half = head_count // 2
    chunk = rows // head_count
    per = chunk // BLK
    high, low = head // half, head % half

    def half_order(which):
        starts = [(which * half + (low ^ k)) * per for k in range(half - 1, -1, -1)]
        return jnp.concatenate([s + jnp.arange(per, dtype=jnp.int32) for s in starts])

    orders = [half_order(1 - high), half_order(high)]
    parts = [
        [part_stage(UNIT, order, table[run], wides[run], kvs, states[run]) for run in range(1, ctx_count)]
        for order in orders
    ]
    others = [[shift(p, "ctx", d + 1) for d, p in enumerate(ps)] for ps in parts]
    mine_table = lax.optimization_barrier((table[0], parts[1]))[0]
    state = stage(UNIT, mine_table, wides[0], kvs, states[0])

    def half_sum(which):
        out = last_stage(orders[which], state, near, gates, others[which])
        share = jnp.dot(out, w_out, preferred_element_type=F32)
        size = chunk // PIECES
        pieces = [share[k * size : (k + 1) * size].astype(BF) for k in range(PIECES)]
        other = jnp.concatenate([swap(piece, "head", 1) for piece in pieces], axis=0)
        return share[chunk:] + other.astype(F32)

    away = half_sum(0)
    away = away.astype(BF)
    back = swap(away, "head", half)
    orders[1] = lax.optimization_barrier((orders[1], away))[0]
    mine = half_sum(1)
    return (mine + back.astype(F32)).astype(BF).reshape(1, chunk, DM)


def solution(mesh):
    wraps = mesh.size >= 128
    return jax.shard_map(
        functools.partial(shards, wraps),
        mesh=mesh,
        in_specs=(
            P("sib", "ctx", "head", None),
            P("sib", "ctx", "head", None),
            P(("sib", "ctx"), "head", None),
            P(),
            P("sib", "ctx", "head", None),
            P("sib", "ctx", "head", None),
            P("sib"),
            P("head", None),
        ),
        out_specs=P("sib", ("ctx", "head"), None),
        check_vma=False,
    )
```

```python
import functools

import jax
import jax.numpy as jnp
from jax import lax
from jax.experimental import pallas as pl
from jax.experimental.pallas import tpu as pltpu
from jax.sharding import PartitionSpec as P

DK = 192
DV = 128
HQ = 8
DM = 2560
BLK = 64
W = 512
LANES = 128
TAIL = DK - LANES
EXT = 2 * LANES
ROWS = BLK + BLK // 2 + BLK
UNIT = 4
NOTES = 16
PIECES = 2
SCALE = DK ** (-0.5)
LOW = -1e30
VMEM = 32 * 1024 * 1024
BF = jnp.bfloat16
F32 = jnp.float32


def params(**more):
    return pltpu.CompilerParams(vmem_limit_bytes=VMEM, **more)


def cost(microseconds):
    return pl.CostEstimate(flops=int(microseconds * 1e9), bytes_accessed=0, transcendentals=0)


def lane_is_low(shape):
    return lax.broadcasted_iota(jnp.int32, shape, len(shape) - 1) < TAIL


def pack_kernel(kv_ref, pool_ref, packed_ref, comp_ref):
    tokens = kv_ref.shape[1]
    pool_key, pool_value = (
        jnp.broadcast_to(pool_ref[k : k + 1, :], (LANES, BLK)).T for k in range(2)
    )
    half = BLK // 2
    pool_tail = jnp.where(lane_is_low((half, LANES)), pool_key[:half], pool_key[half:])
    rows = []
    for tile in range(tokens // LANES):
        part = kv_ref[:, tile * LANES : (tile + 1) * LANES].astype(F32)
        keys = part[:LANES].T
        ends = part[LANES:DK]
        ends = jnp.concatenate([ends, pltpu.roll(ends, LANES - half, 1)], axis=0).T
        values = part[DK:].T
        for sub in range(LANES // BLK):
            base = (tile * (LANES // BLK) + sub) * ROWS
            at = sub * BLK
            key, end, value = keys[at : at + BLK], ends[at : at + half], values[at : at + BLK]
            packed_ref[base : base + BLK] = key.astype(BF)
            packed_ref[base + BLK : base + BLK + half] = end.astype(BF)
            packed_ref[base + BLK + half : base + ROWS] = value.astype(BF)
            comp_key = jnp.sum(key * pool_key, axis=0, keepdims=True)
            comp_end = jnp.sum(end * pool_tail, axis=0, keepdims=True)
            comp_end = comp_end + pltpu.roll(comp_end, TAIL, 1)
            comp_end = jnp.where(lane_is_low((1, LANES)), comp_end, 0.0)
            comp_value = jnp.sum(value * pool_value, axis=0, keepdims=True)
            rows.append(jnp.concatenate([comp_key, comp_end, comp_value], axis=1))
    comp_ref[...] = jnp.concatenate(rows, axis=0).astype(BF)


def pack(kv_t, pooling):
    depth, tokens = kv_t.shape
    blocks = tokens // BLK
    part = NOTES
    return pl.pallas_call(
        pack_kernel,
        grid=(blocks // part,),
        in_specs=[
            pl.BlockSpec((depth, part * BLK), lambda i: (0, i)),
            pl.BlockSpec(pooling.shape, lambda i: (0, 0)),
        ],
        out_specs=(
            pl.BlockSpec((part * ROWS, LANES), lambda i: (i, 0)),
            pl.BlockSpec((part, EXT + DV), lambda i: (i, 0)),
        ),
        out_shape=(
            jax.ShapeDtypeStruct((blocks * ROWS, LANES), BF),
            jax.ShapeDtypeStruct((blocks, EXT + DV), BF),
        ),
        compiler_params=pltpu.CompilerParams(vmem_limit_bytes=2 * VMEM - 4 * 1024 * 1024),
        cost_estimate=cost(5),
        name="pack",
    )(kv_t, pooling)


def wide_queries_kernel(q_ref, out_ref):
    low = lane_is_low((BLK, LANES))
    for pair in range(HQ // 2):
        at = pair * 2 * DK
        first, middle, last = (
            q_ref[:, at + k * LANES : at + (k + 1) * LANES].astype(F32) for k in range(3)
        )
        middle_swap = pltpu.roll(middle, TAIL, 1)
        last_swap = pltpu.roll(last, TAIL, 1)
        top = pair * 2 * BLK
        out_ref[0, top : top + BLK, :LANES] = first.astype(BF)
        out_ref[0, top : top + BLK, LANES:] = jnp.where(low, middle, middle_swap).astype(BF)
        top += BLK
        out_ref[0, top : top + BLK, :LANES] = jnp.where(low, middle_swap, last_swap).astype(BF)
        out_ref[0, top : top + BLK, LANES:] = jnp.where(low, last_swap, last).astype(BF)


def wide_queries(queries):
    rows = queries.shape[0]
    return pl.pallas_call(
        wide_queries_kernel,
        grid=(rows // BLK,),
        in_specs=[pl.BlockSpec((BLK, HQ * DK), lambda i: (i, 0))],
        out_specs=pl.BlockSpec((1, HQ * BLK, EXT), lambda i: (i, 0, 0)),
        out_shape=jax.ShapeDtypeStruct((rows // BLK, HQ * BLK, EXT), BF),
        compiler_params=params(),
        cost_estimate=cost(6),
        name="wide_queries",
    )(queries)


def scores_of(keys, queries):
    return lax.dot_general(keys, queries, (((1,), (1,)), ((), ())), preferred_element_type=F32)


def near_kernel(begin_ref, q_ref, far_ref, own_ref, comp_ref, gate_ref, out_ref, key_ref, value_ref):
    step = pl.program_id(0)
    rows = own_ref.shape[1]

    @pl.when(step == 0)
    def _():
        zeros = jnp.zeros((LANES, TAIL), BF)
        for source, top in ((far_ref, 0), (own_ref, rows)):
            for at in range(0, rows, LANES):
                part = source[:DK, at : at + LANES].astype(F32)
                key_ref[top + at : top + at + LANES, :LANES] = part[:LANES].T.astype(BF)
                end = jnp.concatenate([part[LANES:], jnp.zeros((TAIL, LANES), F32)], axis=0)
                key_ref[top + at : top + at + LANES, LANES:] = end.T.astype(BF)
            value_ref[:, top : top + rows] = source[DK:, :]

    queries = q_ref[0]
    gates = gate_ref[0]
    total_lanes = queries.shape[0]
    scores = scores_of(comp_ref[:, :EXT], queries)
    top = jnp.max(scores, axis=0, keepdims=True)
    weights = jnp.exp((scores - top) * SCALE)
    total = jnp.sum(weights, axis=0, keepdims=True)
    comp_out = lax.dot_general(
        comp_ref[:, EXT:], weights.astype(BF), (((0,), (0,)), ((), ())), preferred_element_type=F32
    )
    out = comp_out * (gates[0:1] / total)

    span = W + LANES
    start = pl.multiple_of((step // 2) * LANES + rows - W, LANES)
    scores = scores_of(key_ref[pl.ds(start, span), :], queries)
    key_pos = start - rows + lax.broadcasted_iota(jnp.int32, (span, total_lanes), 0)
    query_pos = step * BLK + (lax.broadcasted_iota(jnp.int32, (span, total_lanes), 1) & (BLK - 1))
    visible = (key_pos <= query_pos) & (key_pos > query_pos - W) & (key_pos + begin_ref[0] >= 0)
    scores = jnp.where(visible, scores, LOW)
    top = jnp.max(scores, axis=0, keepdims=True)
    weights = jnp.exp((scores - top) * SCALE)
    total = jnp.sum(weights, axis=0, keepdims=True)
    window_out = jnp.dot(
        value_ref[:, pl.ds(start, span)], weights.astype(BF), preferred_element_type=F32
    )
    out_ref[0] = out + window_out * (gates[2:3] / total)


def near_parts(begin, wide, far_t, own_t, comp, gates):
    steps, lanes, _ = wide.shape
    rows = own_t.shape[1]
    whole = lambda array: pl.BlockSpec(array.shape, lambda i, *_: (0,) * array.ndim)
    return pl.pallas_call(
        near_kernel,
        grid_spec=pltpu.PrefetchScalarGridSpec(
            num_scalar_prefetch=1,
            grid=(steps,),
            in_specs=[
                pl.BlockSpec((1, lanes, EXT), lambda i, *_: (i, 0, 0)),
                whole(far_t),
                whole(own_t),
                whole(comp),
                pl.BlockSpec((1, 3, lanes), lambda i, *_: (i, 0, 0)),
            ],
            out_specs=pl.BlockSpec((1, DV, lanes), lambda i, *_: (i, 0, 0)),
            scratch_shapes=[pltpu.VMEM((2 * rows, EXT), BF), pltpu.VMEM((DV, 2 * rows), BF)],
        ),
        out_shape=jax.ShapeDtypeStruct((steps, DV, lanes), F32),
        compiler_params=params(),
        cost_estimate=cost(14),
        name="near",
    )(begin, wide, far_t, own_t, comp, gates)


def add_selected(unit, list_ref, block, q_ref, kv_refs, top, total, acc_ref, key_ref, value_ref):
    count = list_ref[block, list_ref.shape[1] - 1]
    held = kv_refs[0].shape[0]
    half = BLK // 2
    low = lane_is_low((half, LANES))

    def step(index, state):
        top, total = state
        for k in range(unit):
            entry = list_ref[block, jnp.minimum(index * unit + k, count - 1)]
            for place, kv_ref in enumerate(kv_refs):
                inside = (entry >= place * held) & (entry < (place + 1) * held)

                @pl.when(inside)
                def _(kv_ref=kv_ref, place=place):
                    base = pl.multiple_of(entry - place * held, 32)
                    to = k * BLK
                    key_ref[to : to + BLK, :LANES] = kv_ref[pl.ds(base, BLK), :]
                    end = kv_ref[pl.ds(base + BLK, half), :]
                    zero = jnp.zeros_like(end)
                    key_ref[to : to + half, LANES:] = jnp.where(low, end, zero)
                    key_ref[to + half : to + BLK, LANES:] = jnp.where(low, zero, end)
                    value_ref[to : to + BLK, :] = kv_ref[pl.ds(base + BLK + half, BLK), :]

        keys = unit * BLK
        scores = scores_of(key_ref[:keys], q_ref[0])
        row = lax.broadcasted_iota(jnp.int32, scores.shape, 0)
        scores = jnp.where(row < (count - index * unit) * BLK, scores, LOW)
        new_top = jnp.maximum(top, jnp.max(scores, axis=0, keepdims=True))
        weights = jnp.exp((scores - new_top) * SCALE)
        keep = jnp.exp((top - new_top) * SCALE)
        total = total * keep + jnp.sum(weights, axis=0, keepdims=True)
        acc_ref[...] = acc_ref[...] * keep + lax.dot_general(
            value_ref[:keys],
            weights.astype(BF),
            (((0,), (0,)), ((), ())),
            preferred_element_type=F32,
        )
        return new_top, total

    return lax.fori_loop(0, (count + unit - 1) // unit, step, (top, total))


def scratch(unit):
    return [pltpu.VMEM((unit * BLK, EXT), BF), pltpu.VMEM((unit * BLK, DV), BF)]


def whole_spec(array):
    return pl.BlockSpec(array.shape, lambda i, *_: (0,) * array.ndim)


def stage_kernel(first, n_kv, unit, list_ref, q_ref, *refs):
    kv_refs, refs = refs[:n_kv], refs[n_kv:]
    lanes = q_ref.shape[1]
    if first:
        state_out, acc_out, key_ref, value_ref = refs
        top = jnp.full((1, lanes), LOW, F32)
        total = jnp.zeros((1, lanes), F32)
        acc_out[...] = jnp.zeros_like(acc_out)
    else:
        state_in, acc_in, state_out, acc_out, key_ref, value_ref = refs
        top, total = state_in[0, 0:1], state_in[0, 1:2]
        acc_out[...] = acc_in[...]
    top, total = add_selected(
        unit, list_ref, pl.program_id(0), q_ref, kv_refs, top, total, acc_out.at[0], key_ref, value_ref
    )
    state_out[0, 0:1] = top
    state_out[0, 1:2] = total


def stage(unit, lists, wide, kvs, state):
    steps, lanes, _ = wide.shape
    row = pl.BlockSpec((1, 2, lanes), lambda i, *_: (i, 0, 0))
    wide_row = pl.BlockSpec((1, DV, lanes), lambda i, *_: (i, 0, 0))
    in_specs = [pl.BlockSpec((1, lanes, EXT), lambda i, *_: (i, 0, 0))]
    in_specs += [whole_spec(kv) for kv in kvs]
    first = state is None
    aliases = {}
    if not first:
        in_specs += [row, wide_row]
        aliases = {2 + len(kvs): 0, 3 + len(kvs): 1}
    return pl.pallas_call(
        functools.partial(stage_kernel, first, len(kvs), unit),
        grid_spec=pltpu.PrefetchScalarGridSpec(
            num_scalar_prefetch=1,
            grid=(steps,),
            in_specs=in_specs,
            out_specs=[row, wide_row],
            scratch_shapes=scratch(unit),
        ),
        out_shape=(
            jax.ShapeDtypeStruct((steps, 2, lanes), F32),
            jax.ShapeDtypeStruct((steps, DV, lanes), F32),
        ),
        input_output_aliases=aliases,
        compiler_params=params(),
        cost_estimate=cost(9),
        name="stage",
    )(lists, wide, *kvs, *(() if first else state))


def log_total(top, total):
    return jnp.where(total > 0, top * SCALE + jnp.log(jnp.maximum(total, 1e-30)), LOW)


def part_kernel(n_kv, unit, order_ref, list_ref, q_ref, *refs):
    kv_refs, refs = refs[:n_kv], refs[n_kv:]
    state_in, acc_in, out_ref, acc_ref, notes_ref, key_ref, value_ref = refs
    acc_ref[...] = acc_in[0]
    top, total = add_selected(
        unit,
        list_ref,
        order_ref[pl.program_id(0)],
        q_ref,
        kv_refs,
        state_in[0, 0:1],
        state_in[0, 1:2],
        acc_ref,
        key_ref,
        value_ref,
    )
    step, steps = pl.program_id(0), pl.num_programs(0)
    at = pl.multiple_of(step * DV, DV)
    out_ref[pl.ds(at, DV), :] = (acc_ref[...] / jnp.maximum(total, 1e-30)).astype(BF)
    rest = log_total(top, total)
    row = lax.broadcasted_iota(jnp.int32, notes_ref.shape, 0)
    notes = jnp.where(step == 0, 0.0, notes_ref[...])
    for term in range(3):
        value = rest.astype(BF).astype(F32)
        notes = jnp.where(row == term * steps + step, value, notes)
        rest = rest - value
    notes_ref[...] = notes
    out_ref[out_ref.shape[0] - notes.shape[0] :, :] = notes.astype(BF)


def part_stage(unit, order, lists, wide, kvs, state):
    _, lanes, _ = wide.shape
    (steps,) = order.shape
    notes = -(-3 * steps // NOTES) * NOTES
    at = lambda i, order, *_: (order[i], 0, 0)
    return pl.pallas_call(
        functools.partial(part_kernel, len(kvs), unit),
        grid_spec=pltpu.PrefetchScalarGridSpec(
            num_scalar_prefetch=2,
            grid=(steps,),
            in_specs=[pl.BlockSpec((1, lanes, EXT), at)]
            + [whole_spec(kv) for kv in kvs]
            + [pl.BlockSpec((1, 2, lanes), at), pl.BlockSpec((1, DV, lanes), at)],
            out_specs=pl.BlockSpec((steps * DV + notes, lanes), lambda i, *_: (0, 0)),
            scratch_shapes=[pltpu.VMEM((DV, lanes), F32), pltpu.VMEM((notes, lanes), F32)]
            + scratch(unit),
        ),
        out_shape=jax.ShapeDtypeStruct((steps * DV + notes, lanes), BF),
        compiler_params=params(),
        cost_estimate=cost(4),
        name="part_stage",
    )(order, lists, wide, *kvs, *state)


def last_kernel(order_ref, state_ref, acc_ref, near_ref, gate_ref, *refs):
    part_refs, out_ref = refs[:-1], refs[-1]
    total = state_ref[0, 1:2]
    logs = [log_total(state_ref[0, 0:1], total)]
    step, steps = pl.program_id(0), pl.num_programs(0)
    at = pl.multiple_of(step * DV, DV)
    for part_ref in part_refs:
        notes = part_ref[part_ref.shape[0] // DV * DV :, :].astype(F32)
        row = lax.broadcasted_iota(jnp.int32, notes.shape, 0)
        here = functools.reduce(jnp.logical_or, [row == term * steps + step for term in range(3)])
        logs.append(jnp.sum(jnp.where(here, notes, 0.0), axis=0, keepdims=True))
    peak = functools.reduce(jnp.maximum, logs)
    shares = [jnp.exp(log - peak) for log in logs]
    gate = gate_ref[0, 1:2] / functools.reduce(jnp.add, shares)
    out = near_ref[0] + acc_ref[0] * (gate * shares[0] / jnp.maximum(total, 1e-30))
    for share, part_ref in zip(shares[1:], part_refs):
        out = out + part_ref[pl.ds(at, DV), :].astype(F32) * (gate * share)
    for head in range(0, HQ, 2):
        pair = out[:, head * BLK : (head + 2) * BLK].T.astype(BF)
        out_ref[:, head * DV : (head + 1) * DV] = pair[:BLK]
        out_ref[:, (head + 1) * DV : (head + 2) * DV] = pair[BLK:]


def last_stage(order, state, near, gates, others):
    lanes = near.shape[2]
    (steps,) = order.shape
    at = lambda i, order: (order[i], 0, 0)
    return pl.pallas_call(
        last_kernel,
        grid_spec=pltpu.PrefetchScalarGridSpec(
            num_scalar_prefetch=1,
            grid=(steps,),
            in_specs=[
                pl.BlockSpec((1, 2, lanes), at),
                pl.BlockSpec((1, DV, lanes), at),
                pl.BlockSpec((1, DV, lanes), at),
                pl.BlockSpec((1, 3, lanes), at),
            ]
            + [pl.BlockSpec(other.shape, lambda i, order: (0, 0)) for other in others],
            out_specs=pl.BlockSpec((BLK, HQ * DV), lambda i, order: (i, 0)),
        ),
        out_shape=jax.ShapeDtypeStruct((steps * BLK, HQ * DV), BF),
        compiler_params=params(),
        cost_estimate=cost(5),
        name="last_stage",
    )(order, *state, near, gates, *others)


def held_lists(ids, owners, held):
    top_k = ids.shape[-1]
    owner = ids // held
    entry = (ids % held) * ROWS
    match = jnp.zeros(ids.shape, jnp.bool_)
    for place, one in enumerate(owners):
        here = owner == one
        match = match | here
        entry = entry + jnp.where(here, place * held * ROWS, 0)
    slot = jnp.arange(top_k, dtype=jnp.int32)
    before = (slot[:, None] < slot[None, :]) & match[..., :, None]
    rank = jnp.sum(before.astype(jnp.int32), axis=-2)
    rank = jnp.where(match, rank, -1)
    front = jnp.sum(jnp.where(rank[..., :, None] == slot, entry[..., :, None], 0), axis=-2)
    count = jnp.sum(match.astype(jnp.int32), axis=-1, keepdims=True)
    return jnp.concatenate([front, count], axis=-1).astype(jnp.int32)


def swap(value, axis, bit):
    return lax.ppermute(value, axis, [(i, i ^ bit) for i in range(lax.axis_size(axis))])


def shift(value, axis, steps):
    count = lax.axis_size(axis)
    return lax.ppermute(value, axis, [(i, (i + steps) % count) for i in range(count)])


def spread(value, axis, wraps):
    count = lax.axis_size(axis)
    reach = [count // 2, (count - 1) // 2] if wraps else [count - 1, count - 1]
    held = [value, value]
    found = []
    for hop in range(1, max(reach) + 1):
        found.append([])
        for side, sign in enumerate((-1, 1)):
            if hop > reach[side]:
                continue
            pairs = []
            for source in range(count):
                target = source + sign
                if wraps:
                    pairs.append((source, target % count))
                elif 0 <= target < count and 0 <= target - sign * hop < count:
                    pairs.append((source, target))
            held[side] = lax.ppermute(held[side], axis, pairs)
            found[-1].append((held[side], -sign * hop))
    return found


def shards(wraps, queries, suffix_kv, prefix_kv, pooling, gate_logits, selected, lengths, w_out):
    rows = queries.shape[1]
    sib_count, ctx_count, head_count = (lax.axis_size(a) for a in ("sib", "ctx", "head"))
    blocks = rows // BLK
    sib, ctx, head = (lax.axis_index(a) for a in ("sib", "ctx", "head"))
    held_blocks = prefix_kv.shape[0] // BLK

    flat = queries.reshape(rows, HQ * DK)
    ids = selected.reshape(blocks, -1)
    packed, comp = pack(prefix_kv[:, 0, :].T, pooling)
    run_ids = [ids] + [shift(ids, "ctx", -d) for d in range(1, ctx_count)]
    bit = 1
    while bit < ctx_count:
        comp = jnp.concatenate([comp, swap(comp, "ctx", bit)], axis=0)
        bit *= 2
    flat, own_t, _ = lax.optimization_barrier((flat, suffix_kv[0, :, 0, :].T, comp))
    flats = [flat] + [shift(flat, "ctx", -d) for d in range(1, ctx_count)]
    far_t = lax.ppermute(own_t, "ctx", [(i, i + 1) for i in range(ctx_count - 1)])

    hops = [[(packed, 0)]] + spread(packed, "sib", wraps)
    for number, bit in enumerate(1 << k for k in range((sib_count - 1).bit_length())):
        got = swap(comp, "sib", bit)
        behind = [a for a, _ in hops[min(number + 1, len(hops) - 1)]]
        comp, got = lax.optimization_barrier((comp, got, behind))[:2]
        comp = jnp.concatenate([comp, got], axis=0)

    def owner_of(steps):
        other = sib + steps
        if wraps:
            other = other % sib_count
        good = (other >= 0) & (other < sib_count)
        return jnp.where(good, other * ctx_count + ctx, -2)

    levels = [hops[0] + hops[1]] + hops[2:]
    lists = [held_lists(jnp.stack(run_ids), [owner_of(t) for _, t in level], held_blocks) for level in levels]

    begin = (ctx * rows).astype(jnp.int32)
    gates = jax.nn.sigmoid(gate_logits.reshape(rows, 3, HQ))
    alive = begin + jnp.arange(rows, dtype=jnp.int32) < lengths[0]
    gates = jnp.where(alive[:, None, None], gates, 0.0)
    gates = gates.reshape(blocks, BLK, 3, HQ).transpose(0, 2, 3, 1).reshape(blocks, 3, HQ * BLK)

    wides = [wide_queries(f) for f in flats]
    near = near_parts(begin.reshape(1), wides[0], far_t, own_t, comp, gates)
    states = [None] * ctx_count
    for level, table in zip(levels[:-1], lists[:-1]):
        unit = UNIT * min(len(level) - 1, 2)
        for run in range(ctx_count):
            states[run] = stage(unit, table[run], wides[run], [a for a, _ in level], states[run])
    table = lax.optimization_barrier((lists[-1], near, states))[0]
    kvs = [a for a, _ in levels[-1]]

    half = head_count // 2
    chunk = rows // head_count
    per = chunk // BLK
    high, low = head // half, head % half

    def half_order(which):
        starts = [(which * half + (low ^ k)) * per for k in range(half - 1, -1, -1)]
        return jnp.concatenate([s + jnp.arange(per, dtype=jnp.int32) for s in starts])

    orders = [half_order(1 - high), half_order(high)]
    parts = [
        [part_stage(UNIT, order, table[run], wides[run], kvs, states[run]) for run in range(1, ctx_count)]
        for order in orders
    ]
    others = [[shift(p, "ctx", d + 1) for d, p in enumerate(ps)] for ps in parts]
    mine_table = lax.optimization_barrier((table[0], parts[1]))[0]
    state = stage(UNIT, mine_table, wides[0], kvs, states[0])

    def half_sum(which):
        out = last_stage(orders[which], state, near, gates, others[which])
        share = jnp.dot(out, w_out, preferred_element_type=F32)
        size = chunk // PIECES
        pieces = [share[k * size : (k + 1) * size].astype(BF) for k in range(PIECES)]
        other = jnp.concatenate([swap(piece, "head", 1) for piece in pieces], axis=0)
        return share[chunk:] + other.astype(F32)

    away = half_sum(0)
    away = away.astype(BF)
    back = swap(away, "head", half)
    orders[1] = lax.optimization_barrier((orders[1], away))[0]
    mine = half_sum(1)
    return (mine + back.astype(F32)).astype(BF).reshape(1, chunk, DM)


def solution(mesh):
    wraps = mesh.size >= 128
    return jax.shard_map(
        functools.partial(shards, wraps),
        mesh=mesh,
        in_specs=(
            P("sib", "ctx", "head", None),
            P("sib", "ctx", "head", None),
            P(("sib", "ctx"), "head", None),
            P(),
            P("sib", "ctx", "head", None),
            P("sib", "ctx", "head", None),
            P("sib"),
            P("head", None),
        ),
        out_specs=P("sib", ("ctx", "head"), None),
        check_vma=False,
    )
```

```python
import functools

import jax
import jax.numpy as jnp
from jax import lax
from jax.experimental import pallas as pl
from jax.experimental.pallas import tpu as pltpu
from jax.sharding import PartitionSpec as P

DK = 192
DV = 128
HQ = 8
DM = 2560
BLK = 64
W = 512
LANES = 128
TAIL = DK - LANES
EXT = 2 * LANES
ROWS = BLK + BLK // 2 + BLK
UNIT = 4
NOTES = 16
PIECES = 2
SCALE = DK ** (-0.5)
LOW = -1e30
VMEM = 32 * 1024 * 1024
BF = jnp.bfloat16
F32 = jnp.float32


def params(**more):
    return pltpu.CompilerParams(vmem_limit_bytes=VMEM, **more)


def cost(microseconds):
    return pl.CostEstimate(flops=int(microseconds * 1e9), bytes_accessed=0, transcendentals=0)


def lane_is_low(shape):
    return lax.broadcasted_iota(jnp.int32, shape, len(shape) - 1) < TAIL


def pack_kernel(kv_ref, pool_ref, packed_ref, comp_ref):
    tokens = kv_ref.shape[1]
    pool_key, pool_value = (
        jnp.broadcast_to(pool_ref[k : k + 1, :], (LANES, BLK)).T for k in range(2)
    )
    half = BLK // 2
    pool_tail = jnp.where(lane_is_low((half, LANES)), pool_key[:half], pool_key[half:])
    rows = []
    for tile in range(tokens // LANES):
        part = kv_ref[:, tile * LANES : (tile + 1) * LANES].astype(F32)
        keys = part[:LANES].T
        ends = part[LANES:DK]
        ends = jnp.concatenate([ends, pltpu.roll(ends, LANES - half, 1)], axis=0).T
        values = part[DK:].T
        for sub in range(LANES // BLK):
            base = (tile * (LANES // BLK) + sub) * ROWS
            at = sub * BLK
            key, end, value = keys[at : at + BLK], ends[at : at + half], values[at : at + BLK]
            packed_ref[base : base + BLK] = key.astype(BF)
            packed_ref[base + BLK : base + BLK + half] = end.astype(BF)
            packed_ref[base + BLK + half : base + ROWS] = value.astype(BF)
            comp_key = jnp.sum(key * pool_key, axis=0, keepdims=True)
            comp_end = jnp.sum(end * pool_tail, axis=0, keepdims=True)
            comp_end = comp_end + pltpu.roll(comp_end, TAIL, 1)
            comp_end = jnp.where(lane_is_low((1, LANES)), comp_end, 0.0)
            comp_value = jnp.sum(value * pool_value, axis=0, keepdims=True)
            rows.append(jnp.concatenate([comp_key, comp_end, comp_value], axis=1))
    comp_ref[...] = jnp.concatenate(rows, axis=0).astype(BF)


def pack(kv_t, pooling):
    depth, tokens = kv_t.shape
    blocks = tokens // BLK
    part = NOTES
    return pl.pallas_call(
        pack_kernel,
        grid=(blocks // part,),
        in_specs=[
            pl.BlockSpec((depth, part * BLK), lambda i: (0, i)),
            pl.BlockSpec(pooling.shape, lambda i: (0, 0)),
        ],
        out_specs=(
            pl.BlockSpec((part * ROWS, LANES), lambda i: (i, 0)),
            pl.BlockSpec((part, EXT + DV), lambda i: (i, 0)),
        ),
        out_shape=(
            jax.ShapeDtypeStruct((blocks * ROWS, LANES), BF),
            jax.ShapeDtypeStruct((blocks, EXT + DV), BF),
        ),
        compiler_params=pltpu.CompilerParams(vmem_limit_bytes=2 * VMEM - 4 * 1024 * 1024),
        cost_estimate=cost(5),
        name="pack",
    )(kv_t, pooling)


def wide_queries_kernel(q_ref, out_ref):
    low = lane_is_low((BLK, LANES))
    for pair in range(HQ // 2):
        at = pair * 2 * DK
        first, middle, last = (
            q_ref[:, at + k * LANES : at + (k + 1) * LANES].astype(F32) for k in range(3)
        )
        middle_swap = pltpu.roll(middle, TAIL, 1)
        last_swap = pltpu.roll(last, TAIL, 1)
        top = pair * 2 * BLK
        out_ref[0, top : top + BLK, :LANES] = first.astype(BF)
        out_ref[0, top : top + BLK, LANES:] = jnp.where(low, middle, middle_swap).astype(BF)
        top += BLK
        out_ref[0, top : top + BLK, :LANES] = jnp.where(low, middle_swap, last_swap).astype(BF)
        out_ref[0, top : top + BLK, LANES:] = jnp.where(low, last_swap, last).astype(BF)


def wide_queries(queries):
    rows = queries.shape[0]
    return pl.pallas_call(
        wide_queries_kernel,
        grid=(rows // BLK,),
        in_specs=[pl.BlockSpec((BLK, HQ * DK), lambda i: (i, 0))],
        out_specs=pl.BlockSpec((1, HQ * BLK, EXT), lambda i: (i, 0, 0)),
        out_shape=jax.ShapeDtypeStruct((rows // BLK, HQ * BLK, EXT), BF),
        compiler_params=params(),
        cost_estimate=cost(6),
        name="wide_queries",
    )(queries)


def scores_of(keys, queries):
    return lax.dot_general(keys, queries, (((1,), (1,)), ((), ())), preferred_element_type=F32)


def near_kernel(begin_ref, q_ref, far_ref, own_ref, comp_ref, gate_ref, out_ref, key_ref, value_ref):
    step = pl.program_id(0)
    rows = own_ref.shape[1]

    @pl.when(step == 0)
    def _():
        zeros = jnp.zeros((LANES, TAIL), BF)
        for source, top in ((far_ref, 0), (own_ref, rows)):
            for at in range(0, rows, LANES):
                part = source[:DK, at : at + LANES].astype(F32)
                key_ref[top + at : top + at + LANES, :LANES] = part[:LANES].T.astype(BF)
                end = jnp.concatenate([part[LANES:], jnp.zeros((TAIL, LANES), F32)], axis=0)
                key_ref[top + at : top + at + LANES, LANES:] = end.T.astype(BF)
            value_ref[:, top : top + rows] = source[DK:, :]

    queries = q_ref[0]
    gates = gate_ref[0]
    total_lanes = queries.shape[0]
    scores = scores_of(comp_ref[:, :EXT], queries)
    top = jnp.max(scores, axis=0, keepdims=True)
    weights = jnp.exp((scores - top) * SCALE)
    total = jnp.sum(weights, axis=0, keepdims=True)
    comp_out = lax.dot_general(
        comp_ref[:, EXT:], weights.astype(BF), (((0,), (0,)), ((), ())), preferred_element_type=F32
    )
    out = comp_out * (gates[0:1] / total)

    span = W + LANES
    start = pl.multiple_of((step // 2) * LANES + rows - W, LANES)
    scores = scores_of(key_ref[pl.ds(start, span), :], queries)
    key_pos = start - rows + lax.broadcasted_iota(jnp.int32, (span, total_lanes), 0)
    query_pos = step * BLK + (lax.broadcasted_iota(jnp.int32, (span, total_lanes), 1) & (BLK - 1))
    visible = (key_pos <= query_pos) & (key_pos > query_pos - W) & (key_pos + begin_ref[0] >= 0)
    scores = jnp.where(visible, scores, LOW)
    top = jnp.max(scores, axis=0, keepdims=True)
    weights = jnp.exp((scores - top) * SCALE)
    total = jnp.sum(weights, axis=0, keepdims=True)
    window_out = jnp.dot(
        value_ref[:, pl.ds(start, span)], weights.astype(BF), preferred_element_type=F32
    )
    out_ref[0] = out + window_out * (gates[2:3] / total)


def near_parts(begin, wide, far_t, own_t, comp, gates):
    steps, lanes, _ = wide.shape
    rows = own_t.shape[1]
    whole = lambda array: pl.BlockSpec(array.shape, lambda i, *_: (0,) * array.ndim)
    return pl.pallas_call(
        near_kernel,
        grid_spec=pltpu.PrefetchScalarGridSpec(
            num_scalar_prefetch=1,
            grid=(steps,),
            in_specs=[
                pl.BlockSpec((1, lanes, EXT), lambda i, *_: (i, 0, 0)),
                whole(far_t),
                whole(own_t),
                whole(comp),
                pl.BlockSpec((1, 3, lanes), lambda i, *_: (i, 0, 0)),
            ],
            out_specs=pl.BlockSpec((1, DV, lanes), lambda i, *_: (i, 0, 0)),
            scratch_shapes=[pltpu.VMEM((2 * rows, EXT), BF), pltpu.VMEM((DV, 2 * rows), BF)],
        ),
        out_shape=jax.ShapeDtypeStruct((steps, DV, lanes), F32),
        compiler_params=params(),
        cost_estimate=cost(14),
        name="near",
    )(begin, wide, far_t, own_t, comp, gates)


def add_selected(unit, list_ref, block, q_ref, kv_refs, top, total, acc_ref, key_ref, value_ref):
    count = list_ref[block, list_ref.shape[1] - 1]
    held = kv_refs[0].shape[0]
    half = BLK // 2
    low = lane_is_low((half, LANES))

    def step(index, state):
        top, total = state
        for k in range(unit):
            entry = list_ref[block, jnp.minimum(index * unit + k, count - 1)]
            for place, kv_ref in enumerate(kv_refs):
                inside = (entry >= place * held) & (entry < (place + 1) * held)

                @pl.when(inside)
                def _(kv_ref=kv_ref, place=place):
                    base = pl.multiple_of(entry - place * held, 32)
                    to = k * BLK
                    key_ref[to : to + BLK, :LANES] = kv_ref[pl.ds(base, BLK), :]
                    end = kv_ref[pl.ds(base + BLK, half), :]
                    zero = jnp.zeros_like(end)
                    key_ref[to : to + half, LANES:] = jnp.where(low, end, zero)
                    key_ref[to + half : to + BLK, LANES:] = jnp.where(low, zero, end)
                    value_ref[to : to + BLK, :] = kv_ref[pl.ds(base + BLK + half, BLK), :]

        keys = unit * BLK
        scores = scores_of(key_ref[:keys], q_ref[0])
        row = lax.broadcasted_iota(jnp.int32, scores.shape, 0)
        scores = jnp.where(row < (count - index * unit) * BLK, scores, LOW)
        new_top = jnp.maximum(top, jnp.max(scores, axis=0, keepdims=True))
        weights = jnp.exp((scores - new_top) * SCALE)
        keep = jnp.exp((top - new_top) * SCALE)
        total = total * keep + jnp.sum(weights, axis=0, keepdims=True)
        acc_ref[...] = acc_ref[...] * keep + lax.dot_general(
            value_ref[:keys],
            weights.astype(BF),
            (((0,), (0,)), ((), ())),
            preferred_element_type=F32,
        )
        return new_top, total

    return lax.fori_loop(0, (count + unit - 1) // unit, step, (top, total))


def scratch(unit):
    return [pltpu.VMEM((unit * BLK, EXT), BF), pltpu.VMEM((unit * BLK, DV), BF)]


def whole_spec(array):
    return pl.BlockSpec(array.shape, lambda i, *_: (0,) * array.ndim)


def stage_kernel(first, n_kv, unit, list_ref, q_ref, *refs):
    kv_refs, refs = refs[:n_kv], refs[n_kv:]
    lanes = q_ref.shape[1]
    if first:
        state_out, acc_out, key_ref, value_ref = refs
        top = jnp.full((1, lanes), LOW, F32)
        total = jnp.zeros((1, lanes), F32)
        acc_out[...] = jnp.zeros_like(acc_out)
    else:
        state_in, acc_in, state_out, acc_out, key_ref, value_ref = refs
        top, total = state_in[0, 0:1], state_in[0, 1:2]
        acc_out[...] = acc_in[...]
    top, total = add_selected(
        unit, list_ref, pl.program_id(0), q_ref, kv_refs, top, total, acc_out.at[0], key_ref, value_ref
    )
    state_out[0, 0:1] = top
    state_out[0, 1:2] = total


def stage(unit, lists, wide, kvs, state):
    steps, lanes, _ = wide.shape
    row = pl.BlockSpec((1, 2, lanes), lambda i, *_: (i, 0, 0))
    wide_row = pl.BlockSpec((1, DV, lanes), lambda i, *_: (i, 0, 0))
    in_specs = [pl.BlockSpec((1, lanes, EXT), lambda i, *_: (i, 0, 0))]
    in_specs += [whole_spec(kv) for kv in kvs]
    first = state is None
    aliases = {}
    if not first:
        in_specs += [row, wide_row]
        aliases = {2 + len(kvs): 0, 3 + len(kvs): 1}
    return pl.pallas_call(
        functools.partial(stage_kernel, first, len(kvs), unit),
        grid_spec=pltpu.PrefetchScalarGridSpec(
            num_scalar_prefetch=1,
            grid=(steps,),
            in_specs=in_specs,
            out_specs=[row, wide_row],
            scratch_shapes=scratch(unit),
        ),
        out_shape=(
            jax.ShapeDtypeStruct((steps, 2, lanes), F32),
            jax.ShapeDtypeStruct((steps, DV, lanes), F32),
        ),
        input_output_aliases=aliases,
        compiler_params=params(),
        cost_estimate=cost(9),
        name="stage",
    )(lists, wide, *kvs, *(() if first else state))


def log_total(top, total):
    return jnp.where(total > 0, top * SCALE + jnp.log(jnp.maximum(total, 1e-30)), LOW)


def part_kernel(n_kv, unit, order_ref, list_ref, q_ref, *refs):
    kv_refs, refs = refs[:n_kv], refs[n_kv:]
    state_in, acc_in, out_ref, acc_ref, notes_ref, key_ref, value_ref = refs
    acc_ref[...] = acc_in[0]
    top, total = add_selected(
        unit,
        list_ref,
        order_ref[pl.program_id(0)],
        q_ref,
        kv_refs,
        state_in[0, 0:1],
        state_in[0, 1:2],
        acc_ref,
        key_ref,
        value_ref,
    )
    step, steps = pl.program_id(0), pl.num_programs(0)
    at = pl.multiple_of(step * DV, DV)
    out_ref[pl.ds(at, DV), :] = (acc_ref[...] / jnp.maximum(total, 1e-30)).astype(BF)
    rest = log_total(top, total)
    row = lax.broadcasted_iota(jnp.int32, notes_ref.shape, 0)
    notes = jnp.where(step == 0, 0.0, notes_ref[...])
    for term in range(3):
        value = rest.astype(BF).astype(F32)
        notes = jnp.where(row == term * steps + step, value, notes)
        rest = rest - value
    notes_ref[...] = notes
    out_ref[out_ref.shape[0] - notes.shape[0] :, :] = notes.astype(BF)


def part_stage(unit, order, lists, wide, kvs, state):
    _, lanes, _ = wide.shape
    (steps,) = order.shape
    notes = -(-3 * steps // NOTES) * NOTES
    at = lambda i, order, *_: (order[i], 0, 0)
    return pl.pallas_call(
        functools.partial(part_kernel, len(kvs), unit),
        grid_spec=pltpu.PrefetchScalarGridSpec(
            num_scalar_prefetch=2,
            grid=(steps,),
            in_specs=[pl.BlockSpec((1, lanes, EXT), at)]
            + [whole_spec(kv) for kv in kvs]
            + [pl.BlockSpec((1, 2, lanes), at), pl.BlockSpec((1, DV, lanes), at)],
            out_specs=pl.BlockSpec((steps * DV + notes, lanes), lambda i, *_: (0, 0)),
            scratch_shapes=[pltpu.VMEM((DV, lanes), F32), pltpu.VMEM((notes, lanes), F32)]
            + scratch(unit),
        ),
        out_shape=jax.ShapeDtypeStruct((steps * DV + notes, lanes), BF),
        compiler_params=params(),
        cost_estimate=cost(4),
        name="part_stage",
    )(order, lists, wide, *kvs, *state)


def last_kernel(order_ref, state_ref, acc_ref, near_ref, gate_ref, *refs):
    part_refs, out_ref = refs[:-1], refs[-1]
    total = state_ref[0, 1:2]
    logs = [log_total(state_ref[0, 0:1], total)]
    step, steps = pl.program_id(0), pl.num_programs(0)
    at = pl.multiple_of(step * DV, DV)
    for part_ref in part_refs:
        notes = part_ref[part_ref.shape[0] // DV * DV :, :].astype(F32)
        row = lax.broadcasted_iota(jnp.int32, notes.shape, 0)
        here = functools.reduce(jnp.logical_or, [row == term * steps + step for term in range(3)])
        logs.append(jnp.sum(jnp.where(here, notes, 0.0), axis=0, keepdims=True))
    peak = functools.reduce(jnp.maximum, logs)
    shares = [jnp.exp(log - peak) for log in logs]
    gate = gate_ref[0, 1:2] / functools.reduce(jnp.add, shares)
    out = near_ref[0] + acc_ref[0] * (gate * shares[0] / jnp.maximum(total, 1e-30))
    for share, part_ref in zip(shares[1:], part_refs):
        out = out + part_ref[pl.ds(at, DV), :].astype(F32) * (gate * share)
    for head in range(0, HQ, 2):
        pair = out[:, head * BLK : (head + 2) * BLK].T.astype(BF)
        out_ref[:, head * DV : (head + 1) * DV] = pair[:BLK]
        out_ref[:, (head + 1) * DV : (head + 2) * DV] = pair[BLK:]


def last_stage(order, state, near, gates, others):
    lanes = near.shape[2]
    (steps,) = order.shape
    at = lambda i, order: (order[i], 0, 0)
    return pl.pallas_call(
        last_kernel,
        grid_spec=pltpu.PrefetchScalarGridSpec(
            num_scalar_prefetch=1,
            grid=(steps,),
            in_specs=[
                pl.BlockSpec((1, 2, lanes), at),
                pl.BlockSpec((1, DV, lanes), at),
                pl.BlockSpec((1, DV, lanes), at),
                pl.BlockSpec((1, 3, lanes), at),
            ]
            + [pl.BlockSpec(other.shape, lambda i, order: (0, 0)) for other in others],
            out_specs=pl.BlockSpec((BLK, HQ * DV), lambda i, order: (i, 0)),
        ),
        out_shape=jax.ShapeDtypeStruct((steps * BLK, HQ * DV), BF),
        compiler_params=params(),
        cost_estimate=cost(5),
        name="last_stage",
    )(order, *state, near, gates, *others)


def held_lists(ids, owners, held):
    top_k = ids.shape[-1]
    owner = ids // held
    entry = (ids % held) * ROWS
    match = jnp.zeros(ids.shape, jnp.bool_)
    for place, one in enumerate(owners):
        here = owner == one
        match = match | here
        entry = entry + jnp.where(here, place * held * ROWS, 0)
    slot = jnp.arange(top_k, dtype=jnp.int32)
    before = (slot[:, None] < slot[None, :]) & match[..., :, None]
    rank = jnp.sum(before.astype(jnp.int32), axis=-2)
    rank = jnp.where(match, rank, -1)
    front = jnp.sum(jnp.where(rank[..., :, None] == slot, entry[..., :, None], 0), axis=-2)
    count = jnp.sum(match.astype(jnp.int32), axis=-1, keepdims=True)
    return jnp.concatenate([front, count], axis=-1).astype(jnp.int32)


def swap(value, axis, bit):
    return lax.ppermute(value, axis, [(i, i ^ bit) for i in range(lax.axis_size(axis))])


def shift(value, axis, steps):
    count = lax.axis_size(axis)
    return lax.ppermute(value, axis, [(i, (i + steps) % count) for i in range(count)])


def spread(value, axis, wraps):
    count = lax.axis_size(axis)
    reach = [count // 2, (count - 1) // 2] if wraps else [count - 1, count - 1]
    held = [value, value]
    found = []
    for hop in range(1, max(reach) + 1):
        found.append([])
        for side, sign in enumerate((-1, 1)):
            if hop > reach[side]:
                continue
            pairs = []
            for source in range(count):
                target = source + sign
                if wraps:
                    pairs.append((source, target % count))
                elif 0 <= target < count and 0 <= target - sign * hop < count:
                    pairs.append((source, target))
            held[side] = lax.ppermute(held[side], axis, pairs)
            found[-1].append((held[side], -sign * hop))
    return found


def shards(wraps, queries, suffix_kv, prefix_kv, pooling, gate_logits, selected, lengths, w_out):
    rows = queries.shape[1]
    sib_count, ctx_count, head_count = (lax.axis_size(a) for a in ("sib", "ctx", "head"))
    blocks = rows // BLK
    sib, ctx, head = (lax.axis_index(a) for a in ("sib", "ctx", "head"))
    held_blocks = prefix_kv.shape[0] // BLK

    flat = queries.reshape(rows, HQ * DK)
    ids = selected.reshape(blocks, -1)
    packed, comp = pack(prefix_kv[:, 0, :].T, pooling)
    run_ids = [ids] + [shift(ids, "ctx", -d) for d in range(1, ctx_count)]
    bit = 1
    while bit < ctx_count:
        comp = jnp.concatenate([comp, swap(comp, "ctx", bit)], axis=0)
        bit *= 2
    flat, own_t, _ = lax.optimization_barrier((flat, suffix_kv[0, :, 0, :].T, comp))
    flats = [flat] + [shift(flat, "ctx", -d) for d in range(1, ctx_count)]
    far_t = lax.ppermute(own_t, "ctx", [(i, i + 1) for i in range(ctx_count - 1)])

    hops = [[(packed, 0)]] + spread(packed, "sib", wraps)
    for number, bit in enumerate(1 << k for k in range((sib_count - 1).bit_length())):
        got = swap(comp, "sib", bit)
        behind = [a for a, _ in hops[min(number + 1, len(hops) - 1)]][:1]
        comp, got = lax.optimization_barrier((comp, got, behind))[:2]
        comp = jnp.concatenate([comp, got], axis=0)

    def owner_of(steps):
        other = sib + steps
        if wraps:
            other = other % sib_count
        good = (other >= 0) & (other < sib_count)
        return jnp.where(good, other * ctx_count + ctx, -2)

    levels = [hops[0] + hops[1]] + hops[2:]
    lists = [held_lists(jnp.stack(run_ids), [owner_of(t) for _, t in level], held_blocks) for level in levels]

    begin = (ctx * rows).astype(jnp.int32)
    gates = jax.nn.sigmoid(gate_logits.reshape(rows, 3, HQ))
    alive = begin + jnp.arange(rows, dtype=jnp.int32) < lengths[0]
    gates = jnp.where(alive[:, None, None], gates, 0.0)
    gates = gates.reshape(blocks, BLK, 3, HQ).transpose(0, 2, 3, 1).reshape(blocks, 3, HQ * BLK)

    wides = [wide_queries(f) for f in flats]
    near = near_parts(begin.reshape(1), wides[0], far_t, own_t, comp, gates)
    states = [None] * ctx_count
    for level, table in zip(levels[:-1], lists[:-1]):
        unit = UNIT * min(len(level) - 1, 2)
        for run in range(ctx_count):
            states[run] = stage(unit, table[run], wides[run], [a for a, _ in level], states[run])
    table = lax.optimization_barrier((lists[-1], near, states))[0]
    kvs = [a for a, _ in levels[-1]]

    half = head_count // 2
    chunk = rows // head_count
    per = chunk // BLK
    high, low = head // half, head % half

    def half_order(which):
        starts = [(which * half + (low ^ k)) * per for k in range(half - 1, -1, -1)]
        return jnp.concatenate([s + jnp.arange(per, dtype=jnp.int32) for s in starts])

    orders = [half_order(1 - high), half_order(high)]
    parts = [
        [part_stage(UNIT, order, table[run], wides[run], kvs, states[run]) for run in range(1, ctx_count)]
        for order in orders
    ]
    others = [[shift(p, "ctx", d + 1) for d, p in enumerate(ps)] for ps in parts]
    mine_table = lax.optimization_barrier((table[0], parts[1]))[0]
    state = stage(UNIT, mine_table, wides[0], kvs, states[0])

    def half_sum(which):
        out = last_stage(orders[which], state, near, gates, others[which])
        share = jnp.dot(out, w_out, preferred_element_type=F32)
        size = chunk // PIECES
        pieces = [share[k * size : (k + 1) * size].astype(BF) for k in range(PIECES)]
        other = jnp.concatenate([swap(piece, "head", 1) for piece in pieces], axis=0)
        return share[chunk:] + other.astype(F32)

    away = half_sum(0)
    away = away.astype(BF)
    back = swap(away, "head", half)
    orders[1] = lax.optimization_barrier((orders[1], away))[0]
    mine = half_sum(1)
    return (mine + back.astype(F32)).astype(BF).reshape(1, chunk, DM)


def solution(mesh):
    wraps = mesh.size >= 128
    return jax.shard_map(
        functools.partial(shards, wraps),
        mesh=mesh,
        in_specs=(
            P("sib", "ctx", "head", None),
            P("sib", "ctx", "head", None),
            P(("sib", "ctx"), "head", None),
            P(),
            P("sib", "ctx", "head", None),
            P("sib", "ctx", "head", None),
            P("sib"),
            P("head", None),
        ),
        out_specs=P("sib", ("ctx", "head"), None),
        check_vma=False,
    )
```
